512 devices in a mesh: ctx: 32 (over z, x_lo, core), ch: 16 (over y, x_hi).
Axes of the slice: x: 4 (x_hi: 2, x_lo: 2; x = x_hi * 2 + x_lo), y: 8, z: 8, core: 2. Of those that a mesh axis runs over, the one named last changes fastest.
Arguments:
- q_stream: bfloat16 [8192, 8192], P('ctx', 'ch'), may hold values from -6 to 6
- k_stream: bfloat16 [8192, 8192], P('ctx', 'ch'), may hold values from -50 to 50
- v_stream: bfloat16 [8192, 8192], P('ctx', 'ch'), may hold values from -6 to 6
- filters: float32 [8192, 8192], P('ctx', 'ch'), may hold values from -3 to 3
- norm_gain: float32 [8192], replicated, may hold values from 0.4 to 1.6
Outputs:
- block_out: bfloat16 [8192, 8192], P(('ctx', 'ch'))
The draws below stay inside these ranges and needn't reach their ends.
All inputs are finite; a program needn't handle non-finite values.
Results may differ from the reference program's by a relative error of at most 0.017.
Values may be sent and summed in bfloat16 or wider, within the bound.
No kernel may reach another device: no remote copies, remote signals or barrier semaphores. Data moves between devices by JAX's collectives and lax.ppermute only.
A program may use at most 64 MiB of HBM per device.

```python
import math
import jax
import jax.numpy as jnp
from jax import lax

D = 8192
TOK_DEV = 256
TOKEN_COUNT = 8192


def draw_k_stream(key, part):
    key = jax.random.fold_in(key, 7)
    random_child_keys = jax.random.split(key, 3)
    row_scale = jnp.exp(jax.random.uniform(random_child_keys[0], (TOKEN_COUNT, 1), jnp.float32, math.log(0.3), math.log(3.0)))
    col_scale = jnp.exp(jax.random.uniform(random_child_keys[1], (1, D), jnp.float32, math.log(0.3), math.log(3.0)))
    base_values = jnp.clip(jax.random.normal(random_child_keys[2], (TOKEN_COUNT, D), jnp.float32), -5.0, 5.0)
    return (base_values * row_scale * col_scale).astype(jnp.bfloat16)


def draw_filters(key, part):
    key = jax.random.fold_in(key, 19)
    random_child_keys = jax.random.split(key, 7)
    delay_amounts = jnp.arange(TOKEN_COUNT, dtype=jnp.float32)[:, None]
    selector = jax.random.randint(random_child_keys[0], (1, D), 0, 10)
    slow_mask = selector < 5
    slow_rate = jnp.exp(jax.random.uniform(random_child_keys[1], (1, D), jnp.float32, math.log(0.05), 0.0)) / TOKEN_COUNT
    fast_rate = jnp.exp(jax.random.uniform(random_child_keys[2], (1, D), jnp.float32, math.log(1.0 / 50.0), math.log(1.0 / 15.0)))
    rate_values = jnp.where(slow_mask, slow_rate, fast_rate)
    spike_location = jax.random.randint(random_child_keys[3], (2,), 1, TOKEN_COUNT).astype(jnp.float32)
    spike_multiplier = jax.random.uniform(random_child_keys[4], (2,), jnp.float32, 0.6, 0.8)
    logarithm_decay_curve = -rate_values * delay_amounts
    logarithm_decay_curve = logarithm_decay_curve + jnp.where(delay_amounts >= spike_location[0], jnp.log(spike_multiplier[0]), 0.0)
    logarithm_decay_curve = logarithm_decay_curve + jnp.where(delay_amounts >= spike_location[1], jnp.log(spike_multiplier[1]), 0.0)
    envelope = jnp.exp(logarithm_decay_curve) * jnp.sqrt(-jnp.expm1(-2.0 * rate_values))
    noise_values = jnp.clip(jax.random.normal(random_child_keys[5], (TOKEN_COUNT, D), jnp.float32), -5.0, 5.0)
    late_noise = jnp.clip(jax.random.normal(random_child_keys[6], (TOKEN_COUNT, D), jnp.float32), -5.0, 5.0)
    late_scale = 0.5 / math.sqrt(TOKEN_COUNT - TOK_DEV)
    late_part = jnp.where(jnp.logical_and(delay_amounts >= TOK_DEV, jnp.logical_not(slow_mask)), late_scale * late_noise, 0.0)
    return (noise_values * envelope + late_part).astype(jnp.float32)


def shard_levels(stream_key, extent, cuts, smallest, top_value):
    factor_of, own = 1.0, jax.random.fold_in(stream_key, 6)
    for dim, parts in cuts:
        heights = jnp.exp(jax.random.uniform(jax.random.fold_in(own, dim), (parts,), jnp.float32, smallest / len(cuts), top_value / len(cuts)))
        factor_of = factor_of * jnp.repeat(heights, extent[dim] // parts).reshape([-1 if axis == dim else 1 for axis in range(len(extent))])
    return factor_of


def normal_values(own_key, shape, scale, limit, shards=(), held_as=jnp.bfloat16):
    gain = shard_levels(own_key, shape, shards, -0.22, 0.18) if shards else 1.0
    drawn = jax.random.normal(own_key, shape, jnp.float32) * scale * gain
    return jnp.minimum(jnp.maximum(drawn, -limit), limit).astype(held_as)


def setup_inputs(seed: int = 0) -> dict:
    seeds = jax.random.split(jax.random.key(seed), 6)
    return {
        "q_stream": normal_values(seeds[0], (TOKEN_COUNT, D), 1.0, 6.0, ((0, 32), (1, 16))),
        "k_stream": draw_k_stream(jax.random.fold_in(seeds[5], 71), 0),
        "v_stream": normal_values(seeds[2], (TOKEN_COUNT, D), 1.0, 6.0, ((0, 32), (1, 16))),
        "filters": draw_filters(jax.random.fold_in(seeds[5], 71), 0),
        "norm_gain": jnp.clip(1.0 + 0.12 * jax.random.normal(seeds[4], (D,), jnp.float32), 0.4, 1.6),
    }


def reference(q_stream, k_stream, v_stream, filters, norm_gain):
    mixed_input = k_stream.astype(jnp.float32) * v_stream.astype(jnp.float32)
    groups = 16
    group_width = D // groups

    def regroup(values):
        return jnp.transpose(values.reshape(TOKEN_COUNT, groups, group_width), (1, 0, 2))

    def convolve(pair):
        signal, kernel = pair
        spectrum = jnp.fft.rfft(signal, n=2 * TOKEN_COUNT, axis=0) * jnp.fft.rfft(kernel, n=2 * TOKEN_COUNT, axis=0)
        return jnp.fft.irfft(spectrum, n=2 * TOKEN_COUNT, axis=0)[:TOKEN_COUNT]
    convolved = lax.map(convolve, (regroup(mixed_input), regroup(filters)))
    convolved = jnp.transpose(convolved, (1, 0, 2)).reshape(TOKEN_COUNT, D)
    gated_rows = (q_stream.astype(jnp.float32) * convolved).astype(jnp.bfloat16)
    widened = gated_rows.astype(jnp.float32)
    scaling = lax.rsqrt(lax.optimization_barrier(jnp.mean(widened * widened, axis=1, keepdims=True)) + 1e-05)
    return (widened * scaling * norm_gain).astype(jnp.bfloat16)
```

```python
import functools
import math

import jax
import jax.numpy as jnp
import numpy as np
from jax import lax
from jax.experimental import pallas as pl
from jax.experimental.pallas import tpu as pltpu
from jax.sharding import PartitionSpec as P

BF16 = jnp.bfloat16
F32 = jnp.float32
VMEM_BYTES = 40 * 2**20


def parts_of(table):
    high = table.astype(np.float32).astype(jnp.bfloat16)
    low = (table - high.astype(np.float64)).astype(np.float32).astype(jnp.bfloat16)
    return high, low


def stacked_table(matrix):
    table = np.block([[matrix.real, matrix.imag], [-matrix.imag, matrix.real]])
    high, low = parts_of(table)
    return np.concatenate([high, low], axis=0)


def inner_tables(tok_rows):
    half = np.arange(tok_rows // 2)
    even_turns = 2 * half[:, None] * half[None, :] % tok_rows
    odd_turns = half[:, None] * (2 * half[None, :] + 1) % tok_rows
    even, odd = (
        np.exp(-2j * np.pi * turns / tok_rows) for turns in (even_turns, odd_turns)
    )
    return stacked_table(even), stacked_table(odd), stacked_table(odd.T)


def outer_tables(blocks, tok_rows, lines, order_in, order_out):
    index = np.arange(blocks)
    freqs = np.arange(blocks + 1)
    angle = np.pi * (freqs[:, None] * index[None, :] % (2 * blocks)) / blocks
    forward = np.concatenate([np.cos(angle), -np.sin(angle)[1:blocks]], axis=0)
    weight = np.full((2 * blocks, 1), 2.0 / (2 * blocks * tok_rows))
    weight[0] *= 0.5
    weight[blocks] *= 0.5
    backward = (weight * forward).T
    apart = np.eye(lines)
    return (
        np.concatenate(parts_of(np.kron(forward[:, order_in], apart)), axis=1),
        *parts_of(np.kron(backward[order_out], apart)),
    )


def twist_tables(blocks, tok_rows):
    period = 2 * blocks * tok_rows
    index = np.arange(blocks + 1)[:, None] * np.arange(tok_rows)[None, :] % period
    angle = 2.0 * np.pi * index / period
    return np.cos(angle).astype(np.float32), np.sin(angle).astype(np.float32)


def mix_kernel(order, k_hbm, v_hbm, filters_hbm, out_ref, k_ref, v_ref, filters_ref, sems):
    groups, rows, tok_rows = out_ref.shape
    width = rows // 2
    half = tok_rows // 2
    halves = (slice(0, half), slice(half, tok_rows))
    pairs = [(k_hbm, k_ref), (v_hbm, v_ref)]
    pairs += [(filters_hbm.at[at], filters_ref.at[at]) for at in halves]
    copies = [
        pltpu.make_async_copy(source, target, sems.at[n])
        for n, (source, target) in enumerate(pairs)
    ]
    for copy in copies:
        copy.start()
    copies[0].wait()
    copies[1].wait()
    mixed = (k_ref[...].astype(F32) * v_ref[...].astype(F32)).T
    mixed = mixed.reshape(groups, width, tok_rows).astype(BF16)
    for n, group in enumerate(order):
        out_ref[n, :width] = mixed[group]
    for at, copy in zip(halves, copies[2:]):
        copy.wait()
        taps = filters_ref[at].T.reshape(groups, width, half).astype(BF16)
        for n, group in enumerate(order):
            out_ref[n, width:, at] = taps[group]


def split_parts(values):
    high = values.astype(BF16)
    return high, (values - high.astype(F32)).astype(BF16)


def inner_dft(high, low, table_ref):
    left = jnp.concatenate([high, low, high], axis=1)
    table = table_ref[...]
    right = jnp.concatenate([table[: high.shape[1]], table], axis=0)
    return jnp.dot(left, right, preferred_element_type=F32)


def conv_kernel(
    in_ref, twist_ref, inner_ref, outer_ref, out_ref,
    outer, even_high, even_low, odd_high, odd_low, even, odd,
):
    blocks, rows, tok_rows = in_ref.shape
    width = rows // 2
    half = tok_rows // 2
    first, second = slice(0, half), slice(half, tok_rows)
    lines = 8
    subs = range(width // lines)
    real_rows = (blocks + 1) * lines
    cos_ref, sin_ref = twist_ref.at[0], twist_ref.at[1]
    even_ref, odd_ref, back_ref = (inner_ref.at[n] for n in range(3))
    back_rows = blocks * lines
    high_ref = outer_ref.at[2 * back_rows : 3 * back_rows]
    low_ref = outer_ref.at[3 * back_rows : 4 * back_rows]

    def of_freq(k, start=0):
        return slice(start + k * lines, start + (k + 1) * lines)

    def outer_dft(stream):
        top = stream * width
        whole = in_ref[:, top : top + width].astype(F32)
        for sub in subs:
            data = whole[:, sub * lines : (sub + 1) * lines]
            data = data.reshape(blocks * lines, tok_rows).astype(BF16)
            outer[stream, sub] = jnp.dot(
                outer_ref[: 2 * back_rows],
                jnp.concatenate([data, data], axis=0),
                preferred_element_type=F32,
            )

    def twist(stream):
        for k in range(blocks + 1):
            halves = [[], []]
            turns = [(cos_ref[k : k + 1, at], sin_ref[k : k + 1, at]) for at in (first, second)]
            for sub in subs:
                twisted = []
                for cols, (cos, sin) in zip((first, second), turns):
                    re = outer[stream, sub, of_freq(k), cols]
                    if k == 0:
                        twisted.append((re, jnp.zeros_like(re)))
                        continue
                    if k == blocks:
                        twisted.append((re * cos, -(re * sin)))
                        continue
                    im = outer[stream, sub, of_freq(k - 1, real_rows), cols]
                    twisted.append((re * cos + im * sin, im * cos - re * sin))
                (re_a, im_a), (re_b, im_b) = twisted
                halves[0].append(jnp.concatenate([re_a + re_b, im_a + im_b], axis=1))
                halves[1].append(jnp.concatenate([re_a - re_b, im_a - im_b], axis=1))
            at = slice(k * width, (k + 1) * width)
            for parts, high, low in (
                (halves[0], even_high, even_low),
                (halves[1], odd_high, odd_low),
            ):
                joined = jnp.concatenate(parts, axis=0)
                high[stream, at], low[stream, at] = split_parts(joined)

    outer_dft(0)
    outer_dft(1)
    twist(0)
    sig_even = inner_dft(even_high[0], even_low[0], even_ref)
    sig_odd = inner_dft(odd_high[0], odd_low[0], odd_ref)
    twist(1)
    ker_even = inner_dft(even_high[1], even_low[1], even_ref)
    ker_odd = inner_dft(odd_high[1], odd_low[1], odd_ref)
    for sig, ker, back_table_ref, out in (
        (sig_even, ker_even, even_ref, even),
        (sig_odd, ker_odd, back_ref, odd),
    ):
        sig_re, sig_im = sig[:, first], sig[:, second]
        ker_re, ker_im = ker[:, first], ker[:, second]
        prod_re = sig_re * ker_re - sig_im * ker_im
        prod_neg = -(sig_re * ker_im + sig_im * ker_re)
        product = jnp.concatenate([prod_re, prod_neg], axis=1)
        out[...] = inner_dft(*split_parts(product), back_table_ref)

    for k in range(blocks + 1):
        for cols, sign in ((first, 1), (second, -1)):
            cos, sin = cos_ref[k : k + 1, cols], sin_ref[k : k + 1, cols]
            for sub in subs:
                at = slice(k * width + sub * lines, k * width + (sub + 1) * lines)
                z = even[at] + odd[at] if sign > 0 else even[at] - odd[at]
                re, neg = z[:, first], z[:, second]
                outer[0, sub, of_freq(k), cols] = re * cos + neg * sin
                if 0 < k < blocks:
                    outer[0, sub, of_freq(k - 1, real_rows), cols] = re * sin - neg * cos
    parts = []
    for sub in subs:
        high, low = split_parts(outer[0, sub])
        back = jnp.dot(high_ref[...], low, preferred_element_type=F32)
        back += jnp.dot(low_ref[...], high, preferred_element_type=F32)
        back += jnp.dot(high_ref[...], high, preferred_element_type=F32)
        parts.append(back.reshape(blocks, lines, tok_rows))
    out_ref[...] = jnp.concatenate(parts, axis=1).astype(BF16)


def gate_kernel(order_in, order_out, q_ref, conv_ref, out_ref):
    groups, width, tok_rows = conv_ref.shape
    parts = [conv_ref[order_in.index(group)].astype(F32) for group in range(groups)]
    convolved = jnp.concatenate(parts, axis=0).T
    gated_rows = (q_ref[...].astype(F32) * convolved).astype(BF16)
    tokens = out_ref.shape[1]
    for n, group in enumerate(order_out):
        out_ref[n] = gated_rows[group * tokens : (group + 1) * tokens]


def norm_kernel(order, rows_ref, gain_ref, out_ref):
    groups, _, width = rows_ref.shape
    squares = 0.0
    for n in range(groups):
        widened = rows_ref[n].astype(F32)
        squares = squares + widened * widened
    total = jnp.sum(squares, axis=1, keepdims=True)
    scaling = lax.rsqrt(total / (groups * width) + 1e-05)
    for n, group in enumerate(order):
        cols = slice(group * width, (group + 1) * width)
        row = rows_ref[n].astype(F32)
        out_ref[:, cols] = (row * scaling * gain_ref[:, cols]).astype(BF16)


def on_device(kernel, out_shape, cost, scratch=(), **specs):
    return pl.pallas_call(
        kernel,
        out_shape=out_shape,
        scratch_shapes=list(scratch),
        compiler_params=pltpu.CompilerParams(vmem_limit_bytes=VMEM_BYTES),
        cost_estimate=pl.CostEstimate(
            flops=cost[0], bytes_accessed=cost[1], transcendentals=0
        ),
        **specs,
    )


def mix(k_stream, v_stream, filters, order):
    tok_rows, channels = k_stream.shape
    groups = len(order)
    shape = jax.ShapeDtypeStruct((groups, 2 * channels // groups, tok_rows), BF16)
    cost = (k_stream.size, 12 * k_stream.size)
    scratch = [pltpu.VMEM(k_stream.shape, BF16)] * 2
    scratch += [pltpu.VMEM(k_stream.shape, F32), pltpu.SemaphoreType.DMA((4,))]
    specs = [pl.BlockSpec(memory_space=pltpu.HBM)] * 3
    held = [
        pltpu.with_memory_space_constraint(array, pltpu.HBM)
        for array in (k_stream, v_stream, filters)
    ]
    kernel = functools.partial(mix_kernel, order)
    return on_device(kernel, shape, cost, scratch, in_specs=specs)(*held)


def convolve(pieces, order_in, order_out):
    blocks, rows, tok_rows = pieces.shape
    width = rows // 2
    lines = 8
    tables = (
        np.stack(twist_tables(blocks, tok_rows)),
        np.stack(inner_tables(tok_rows)),
        np.concatenate(
            outer_tables(blocks, tok_rows, lines, order_in, order_out), axis=0
        ),
    )
    shape = jax.ShapeDtypeStruct((blocks, width, tok_rows), BF16)
    freq_rows = (blocks + 1) * width
    scratch = [pltpu.VMEM((2, width // lines, 2 * blocks * lines, tok_rows), F32)]
    scratch += [pltpu.VMEM((2, freq_rows, tok_rows), BF16)] * 4
    scratch += [pltpu.VMEM((freq_rows, tok_rows), F32)] * 2
    cost = (2 * 3 * freq_rows * 3 * 2 * tok_rows * tok_rows, 2 * 2**20)
    return on_device(conv_kernel, shape, cost, scratch)(
        pieces, *(jnp.asarray(table) for table in tables)
    )


def gate(q_stream, convolved, order_in, order_out):
    tok_rows, channels = q_stream.shape
    count = len(order_out)
    shape = jax.ShapeDtypeStruct((count, tok_rows // count, channels), BF16)
    cost = (q_stream.size, 6 * q_stream.size)
    kernel = functools.partial(gate_kernel, order_in, order_out)
    return on_device(kernel, shape, cost)(q_stream, convolved)


def normalize(rows, norm_gain, order):
    groups, tokens, width = rows.shape
    channels = groups * width
    shape = jax.ShapeDtypeStruct((tokens, channels), BF16)
    cost = (6 * tokens * channels, 4 * tokens * channels + 4 * channels)
    kernel = functools.partial(norm_kernel, order)
    return on_device(kernel, shape, cost)(rows, norm_gain.reshape(1, channels))


def exchange(array, axis, order):
    return lax.all_to_all(
        array, axis, split_axis=0, concat_axis=0, axis_index_groups=[order], tiled=True
    )


def spread(planes, lines, places):
    far = [0]
    while len(far) < planes:
        far = [2 * n for n in far] + [2 * n + 1 for n in far]
    first_to_last = [
        (plane * lines + (turn + n) % lines) * places + place
        for place in range(places)
        for turn in range(lines)
        for n, plane in enumerate(far)
    ]
    return first_to_last[::-1]


def local(q_stream, k_stream, v_stream, filters, norm_gain):
    ctx, ch = lax.axis_size("ctx"), lax.axis_size("ch")
    order_ctx = spread(ctx // 4, 2, 2)
    order_ch = spread(ch // 2, 2, 1)
    pieces = exchange(mix(k_stream, v_stream, filters, order_ctx), "ctx", order_ctx)
    convolved = convolve(pieces, order_ctx, order_ctx)
    returned = exchange(convolved, "ctx", order_ctx)
    gated_rows = gate(q_stream, returned, order_ctx, order_ch)
    regrouped = exchange(gated_rows, "ch", order_ch)
    return normalize(regrouped, norm_gain, order_ch)


def solution(mesh):
    return jax.shard_map(
        local,
        mesh=mesh,
        in_specs=(P("ctx", "ch"), P("ctx", "ch"), P("ctx", "ch"), P("ctx", "ch"), P()),
        out_specs=P(("ctx", "ch"), None),
        check_vma=False,
    )
```

```python
import functools
import math

import jax
import jax.numpy as jnp
import numpy as np
from jax import lax
from jax.experimental import pallas as pl
from jax.experimental.pallas import tpu as pltpu
from jax.sharding import PartitionSpec as P

BF16 = jnp.bfloat16
F32 = jnp.float32
VMEM_BYTES = 40 * 2**20


def parts_of(table):
    high = table.astype(np.float32).astype(jnp.bfloat16)
    low = (table - high.astype(np.float64)).astype(np.float32).astype(jnp.bfloat16)
    return high, low


def stacked_table(matrix):
    table = np.block([[matrix.real, matrix.imag], [-matrix.imag, matrix.real]])
    high, low = parts_of(table)
    return np.concatenate([high, low], axis=0)


def inner_tables(tok_rows):
    half = np.arange(tok_rows // 2)
    even_turns = 2 * half[:, None] * half[None, :] % tok_rows
    odd_turns = half[:, None] * (2 * half[None, :] + 1) % tok_rows
    even, odd = (
        np.exp(-2j * np.pi * turns / tok_rows) for turns in (even_turns, odd_turns)
    )
    return stacked_table(even), stacked_table(odd), stacked_table(odd.T)


def outer_tables(blocks, tok_rows, lines, order_in, order_out):
    index = np.arange(blocks)
    freqs = np.arange(blocks + 1)
    angle = np.pi * (freqs[:, None] * index[None, :] % (2 * blocks)) / blocks
    forward = np.concatenate([np.cos(angle), -np.sin(angle)[1:blocks]], axis=0)
    weight = np.full((2 * blocks, 1), 2.0 / (2 * blocks * tok_rows))
    weight[0] *= 0.5
    weight[blocks] *= 0.5
    backward = (weight * forward).T
    apart = np.eye(lines)
    return (
        np.concatenate(parts_of(np.kron(forward[:, order_in], apart)), axis=1),
        *parts_of(np.kron(backward[order_out], apart)),
    )


def twist_tables(blocks, tok_rows):
    period = 2 * blocks * tok_rows
    index = np.arange(blocks + 1)[:, None] * np.arange(tok_rows)[None, :] % period
    angle = 2.0 * np.pi * index / period
    return np.cos(angle).astype(np.float32), np.sin(angle).astype(np.float32)


def mix_kernel(order, k_hbm, v_hbm, filters_hbm, out_ref, k_ref, v_ref, filters_ref, sems):
    groups, rows, tok_rows = out_ref.shape
    width = rows // 2
    half = tok_rows // 2
    halves = (slice(0, half), slice(half, tok_rows))
    pairs = [(k_hbm, k_ref), (v_hbm, v_ref)]
    pairs += [(filters_hbm.at[at], filters_ref.at[at]) for at in halves]
    copies = [
        pltpu.make_async_copy(source, target, sems.at[n])
        for n, (source, target) in enumerate(pairs)
    ]
    for copy in copies:
        copy.start()
    copies[0].wait()
    copies[1].wait()
    mixed = (k_ref[...].astype(F32) * v_ref[...].astype(F32)).T
    mixed = mixed.reshape(groups, width, tok_rows).astype(BF16)
    for n, group in enumerate(order):
        out_ref[n, :width] = mixed[group]
    for at, copy in zip(halves, copies[2:]):
        copy.wait()
        taps = filters_ref[at].T.reshape(groups, width, half).astype(BF16)
        for n, group in enumerate(order):
            out_ref[n, width:, at] = taps[group]


def split_parts(values):
    high = values.astype(BF16)
    return high, (values - high.astype(F32)).astype(BF16)


def inner_dft(high, low, table_ref):
    left = jnp.concatenate([high, low, high], axis=1)
    table = table_ref[...]
    right = jnp.concatenate([table[: high.shape[1]], table], axis=0)
    return jnp.dot(left, right, preferred_element_type=F32)


def conv_kernel(
    in_ref, twist_ref, inner_ref, outer_ref, out_ref,
    outer, even_high, even_low, odd_high, odd_low, even, odd,
):
    blocks, rows, tok_rows = in_ref.shape
    width = rows // 2
    half = tok_rows // 2
    first, second = slice(0, half), slice(half, tok_rows)
    lines = 8
    subs = range(width // lines)
    real_rows = (blocks + 1) * lines
    cos_ref, sin_ref = twist_ref.at[0], twist_ref.at[1]
    even_ref, odd_ref, back_ref = (inner_ref.at[n] for n in range(3))
    back_rows = blocks * lines
    high_ref = outer_ref.at[2 * back_rows : 3 * back_rows]
    low_ref = outer_ref.at[3 * back_rows : 4 * back_rows]

    def of_freq(k, start=0):
        return slice(start + k * lines, start + (k + 1) * lines)

    def outer_dft(stream):
        top = stream * width
        whole = in_ref[:, top : top + width].astype(F32)
        for sub in subs:
            data = whole[:, sub * lines : (sub + 1) * lines]
            data = data.reshape(blocks * lines, tok_rows).astype(BF16)
            outer[stream, sub] = jnp.dot(
                outer_ref[: 2 * back_rows],
                jnp.concatenate([data, data], axis=0),
                preferred_element_type=F32,
            )

    def twist(stream):
        for k in range(blocks + 1):
            halves = [[], []]
            turns = [(cos_ref[k : k + 1, at], sin_ref[k : k + 1, at]) for at in (first, second)]
            for sub in subs:
                twisted = []
                for cols, (cos, sin) in zip((first, second), turns):
                    re = outer[stream, sub, of_freq(k), cols]
                    if k == 0:
                        twisted.append((re, jnp.zeros_like(re)))
                        continue
                    if k == blocks:
                        twisted.append((re * cos, -(re * sin)))
                        continue
                    im = outer[stream, sub, of_freq(k - 1, real_rows), cols]
                    twisted.append((re * cos + im * sin, im * cos - re * sin))
                (re_a, im_a), (re_b, im_b) = twisted
                halves[0].append(jnp.concatenate([re_a + re_b, im_a + im_b], axis=1))
                halves[1].append(jnp.concatenate([re_a - re_b, im_a - im_b], axis=1))
            at = slice(k * width, (k + 1) * width)
            for parts, high, low in (
                (halves[0], even_high, even_low),
                (halves[1], odd_high, odd_low),
            ):
                joined = jnp.concatenate(parts, axis=0)
                high[stream, at], low[stream, at] = split_parts(joined)

    outer_dft(0)
    outer_dft(1)
    twist(0)
    sig_even = inner_dft(even_high[0], even_low[0], even_ref)
    sig_odd = inner_dft(odd_high[0], odd_low[0], odd_ref)
    twist(1)
    ker_even = inner_dft(even_high[1], even_low[1], even_ref)
    ker_odd = inner_dft(odd_high[1], odd_low[1], odd_ref)
    for sig, ker, back_table_ref, out in (
        (sig_even, ker_even, even_ref, even),
        (sig_odd, ker_odd, back_ref, odd),
    ):
        sig_re, sig_im = sig[:, first], sig[:, second]
        ker_re, ker_im = ker[:, first], ker[:, second]
        prod_re = sig_re * ker_re - sig_im * ker_im
        prod_neg = -(sig_re * ker_im + sig_im * ker_re)
        product = jnp.concatenate([prod_re, prod_neg], axis=1)
        out[...] = inner_dft(*split_parts(product), back_table_ref)

    for k in range(blocks + 1):
        for cols, sign in ((first, 1), (second, -1)):
            cos, sin = cos_ref[k : k + 1, cols], sin_ref[k : k + 1, cols]
            for sub in subs:
                at = slice(k * width + sub * lines, k * width + (sub + 1) * lines)
                z = even[at] + odd[at] if sign > 0 else even[at] - odd[at]
                re, neg = z[:, first], z[:, second]
                outer[0, sub, of_freq(k), cols] = re * cos + neg * sin
                if 0 < k < blocks:
                    outer[0, sub, of_freq(k - 1, real_rows), cols] = re * sin - neg * cos
    parts = []
    for sub in subs:
        high, low = split_parts(outer[0, sub])
        back = jnp.dot(high_ref[...], low, preferred_element_type=F32)
        back += jnp.dot(low_ref[...], high, preferred_element_type=F32)
        back += jnp.dot(high_ref[...], high, preferred_element_type=F32)
        parts.append(back.reshape(blocks, lines, tok_rows))
    out_ref[...] = jnp.concatenate(parts, axis=1).astype(BF16)


def gate_kernel(order_in, order_out, q_ref, conv_ref, out_ref):
    groups, width, tok_rows = conv_ref.shape
    parts = [conv_ref[order_in.index(group)].astype(F32) for group in range(groups)]
    convolved = jnp.concatenate(parts, axis=0).T
    gated_rows = (q_ref[...].astype(F32) * convolved).astype(BF16)
    tokens = out_ref.shape[1]
    for n, group in enumerate(order_out):
        out_ref[n] = gated_rows[group * tokens : (group + 1) * tokens]


def norm_kernel(order, rows_ref, gain_ref, out_ref):
    groups, _, width = rows_ref.shape
    squares = 0.0
    for n in range(groups):
        widened = rows_ref[n].astype(F32)
        squares = squares + widened * widened
    total = jnp.sum(squares, axis=1, keepdims=True)
    scaling = lax.rsqrt(total / (groups * width) + 1e-05)
    for n, group in enumerate(order):
        cols = slice(group * width, (group + 1) * width)
        row = rows_ref[n].astype(F32)
        out_ref[:, cols] = (row * scaling * gain_ref[:, cols]).astype(BF16)


def on_device(kernel, out_shape, cost, scratch=(), **specs):
    return pl.pallas_call(
        kernel,
        out_shape=out_shape,
        scratch_shapes=list(scratch),
        compiler_params=pltpu.CompilerParams(vmem_limit_bytes=VMEM_BYTES),
        cost_estimate=pl.CostEstimate(
            flops=cost[0], bytes_accessed=cost[1], transcendentals=0
        ),
        **specs,
    )


def mix(k_stream, v_stream, filters, order):
    tok_rows, channels = k_stream.shape
    groups = len(order)
    shape = jax.ShapeDtypeStruct((groups, 2 * channels // groups, tok_rows), BF16)
    cost = (k_stream.size, 12 * k_stream.size)
    scratch = [pltpu.VMEM(k_stream.shape, BF16)] * 2
    scratch += [pltpu.VMEM(k_stream.shape, F32), pltpu.SemaphoreType.DMA((4,))]
    specs = [pl.BlockSpec(memory_space=pltpu.HBM)] * 3
    held = [
        pltpu.with_memory_space_constraint(array, pltpu.HBM)
        for array in (k_stream, v_stream, filters)
    ]
    kernel = functools.partial(mix_kernel, order)
    return on_device(kernel, shape, cost, scratch, in_specs=specs)(*held)


def convolve(pieces, order_in, order_out):
    blocks, rows, tok_rows = pieces.shape
    width = rows // 2
    lines = 8
    tables = (
        np.stack(twist_tables(blocks, tok_rows)),
        np.stack(inner_tables(tok_rows)),
        np.concatenate(
            outer_tables(blocks, tok_rows, lines, order_in, order_out), axis=0
        ),
    )
    shape = jax.ShapeDtypeStruct((blocks, width, tok_rows), BF16)
    freq_rows = (blocks + 1) * width
    scratch = [pltpu.VMEM((2, width // lines, 2 * blocks * lines, tok_rows), F32)]
    scratch += [pltpu.VMEM((2, freq_rows, tok_rows), BF16)] * 4
    scratch += [pltpu.VMEM((freq_rows, tok_rows), F32)] * 2
    cost = (2 * 3 * freq_rows * 3 * 2 * tok_rows * tok_rows, 2 * 2**20)
    return on_device(conv_kernel, shape, cost, scratch)(
        pieces, *(jnp.asarray(table) for table in tables)
    )


def gate(q_stream, convolved, order_in, order_out):
    tok_rows, channels = q_stream.shape
    count = len(order_out)
    shape = jax.ShapeDtypeStruct((count, tok_rows // count, channels), BF16)
    cost = (q_stream.size, 6 * q_stream.size)
    kernel = functools.partial(gate_kernel, order_in, order_out)
    return on_device(kernel, shape, cost)(q_stream, convolved)


def normalize(rows, norm_gain, order):
    groups, tokens, width = rows.shape
    channels = groups * width
    shape = jax.ShapeDtypeStruct((tokens, channels), BF16)
    cost = (6 * tokens * channels, 4 * tokens * channels + 4 * channels)
    kernel = functools.partial(norm_kernel, order)
    return on_device(kernel, shape, cost)(rows, norm_gain.reshape(1, channels))


def exchange(array, axis, order):
    return lax.all_to_all(
        array, axis, split_axis=0, concat_axis=0, axis_index_groups=[order], tiled=True
    )


def spread(planes, lines, places):
    far = [0]
    while len(far) < planes:
        far = [2 * n for n in far] + [2 * n + 1 for n in far]
    first_to_last = [
        (plane * lines + (turn + n) % lines) * places + place
        for place in range(places)
        for turn in range(lines)
        for n, plane in enumerate(far)
    ]
    return first_to_last[::-1]


def local(q_stream, k_stream, v_stream, filters, norm_gain):
    ctx, ch = lax.axis_size("ctx"), lax.axis_size("ch")
    order_ctx = spread(ctx // 4, 2, 2)
    order_ch = spread(ch // 2, 1, 2)
    pieces = exchange(mix(k_stream, v_stream, filters, order_ctx), "ctx", order_ctx)
    convolved = convolve(pieces, order_ctx, order_ctx)
    returned = exchange(convolved, "ctx", order_ctx)
    gated_rows = gate(q_stream, returned, order_ctx, order_ch)
    regrouped = exchange(gated_rows, "ch", order_ch)
    return normalize(regrouped, norm_gain, order_ch)


def solution(mesh):
    return jax.shard_map(
        local,
        mesh=mesh,
        in_specs=(P("ctx", "ch"), P("ctx", "ch"), P("ctx", "ch"), P("ctx", "ch"), P()),
        out_specs=P(("ctx", "ch"), None),
        check_vma=False,
    )
```

```python
import functools
import math

import jax
import jax.numpy as jnp
import numpy as np
from jax import lax
from jax.experimental import pallas as pl
from jax.experimental.pallas import tpu as pltpu
from jax.sharding import PartitionSpec as P

BF16 = jnp.bfloat16
F32 = jnp.float32
VMEM_BYTES = 40 * 2**20


def parts_of(table):
    high = table.astype(np.float32).astype(jnp.bfloat16)
    low = (table - high.astype(np.float64)).astype(np.float32).astype(jnp.bfloat16)
    return high, low


def stacked_table(matrix):
    table = np.block([[matrix.real, matrix.imag], [-matrix.imag, matrix.real]])
    high, low = parts_of(table)
    return np.concatenate([high, low], axis=0)


def inner_tables(tok_rows):
    half = np.arange(tok_rows // 2)
    even_turns = 2 * half[:, None] * half[None, :] % tok_rows
    odd_turns = half[:, None] * (2 * half[None, :] + 1) % tok_rows
    even, odd = (
        np.exp(-2j * np.pi * turns / tok_rows) for turns in (even_turns, odd_turns)
    )
    return stacked_table(even), stacked_table(odd), stacked_table(odd.T)


def outer_tables(blocks, tok_rows, lines, order_in, order_out):
    index = np.arange(blocks)
    freqs = np.arange(blocks + 1)
    angle = np.pi * (freqs[:, None] * index[None, :] % (2 * blocks)) / blocks
    forward = np.concatenate([np.cos(angle), -np.sin(angle)[1:blocks]], axis=0)
    weight = np.full((2 * blocks, 1), 2.0 / (2 * blocks * tok_rows))
    weight[0] *= 0.5
    weight[blocks] *= 0.5
    backward = (weight * forward).T
    apart = np.eye(lines)
    return (
        np.concatenate(parts_of(np.kron(forward[:, order_in], apart)), axis=1),
        *parts_of(np.kron(backward[order_out], apart)),
    )


def twist_tables(blocks, tok_rows):
    period = 2 * blocks * tok_rows
    index = np.arange(blocks + 1)[:, None] * np.arange(tok_rows)[None, :] % period
    angle = 2.0 * np.pi * index / period
    return np.cos(angle).astype(np.float32), np.sin(angle).astype(np.float32)


def mix_kernel(order, k_hbm, v_hbm, filters_hbm, out_ref, k_ref, v_ref, filters_ref, sems):
    groups, rows, tok_rows = out_ref.shape
    width = rows // 2
    half = tok_rows // 2
    halves = (slice(0, half), slice(half, tok_rows))
    pairs = [(k_hbm, k_ref), (v_hbm, v_ref)]
    pairs += [(filters_hbm.at[at], filters_ref.at[at]) for at in halves]
    copies = [
        pltpu.make_async_copy(source, target, sems.at[n])
        for n, (source, target) in enumerate(pairs)
    ]
    for copy in copies:
        copy.start()
    copies[0].wait()
    copies[1].wait()
    mixed = (k_ref[...].astype(F32) * v_ref[...].astype(F32)).T
    mixed = mixed.reshape(groups, width, tok_rows).astype(BF16)
    for n, group in enumerate(order):
        out_ref[n, :width] = mixed[group]
    for at, copy in zip(halves, copies[2:]):
        copy.wait()
        taps = filters_ref[at].T.reshape(groups, width, half).astype(BF16)
        for n, group in enumerate(order):
            out_ref[n, width:, at] = taps[group]


def split_parts(values):
    high = values.astype(BF16)
    return high, (values - high.astype(F32)).astype(BF16)


def inner_dft(high, low, table_ref):
    left = jnp.concatenate([high, low, high], axis=1)
    table = table_ref[...]
    right = jnp.concatenate([table[: high.shape[1]], table], axis=0)
    return jnp.dot(left, right, preferred_element_type=F32)


def conv_kernel(
    in_ref, twist_ref, inner_ref, outer_ref, out_ref,
    outer, even_high, even_low, odd_high, odd_low, even, odd,
):
    blocks, rows, tok_rows = in_ref.shape
    width = rows // 2
    half = tok_rows // 2
    first, second = slice(0, half), slice(half, tok_rows)
    lines = 8
    subs = range(width // lines)
    real_rows = (blocks + 1) * lines
    cos_ref, sin_ref = twist_ref.at[0], twist_ref.at[1]
    even_ref, odd_ref, back_ref = (inner_ref.at[n] for n in range(3))
    back_rows = blocks * lines
    high_ref = outer_ref.at[2 * back_rows : 3 * back_rows]
    low_ref = outer_ref.at[3 * back_rows : 4 * back_rows]

    def of_freq(k, start=0):
        return slice(start + k * lines, start + (k + 1) * lines)

    def outer_dft(stream):
        top = stream * width
        whole = in_ref[:, top : top + width].astype(F32)
        for sub in subs:
            data = whole[:, sub * lines : (sub + 1) * lines]
            data = data.reshape(blocks * lines, tok_rows).astype(BF16)
            outer[stream, sub] = jnp.dot(
                outer_ref[: 2 * back_rows],
                jnp.concatenate([data, data], axis=0),
                preferred_element_type=F32,
            )

    def twist(stream):
        for k in range(blocks + 1):
            halves = [[], []]
            turns = [(cos_ref[k : k + 1, at], sin_ref[k : k + 1, at]) for at in (first, second)]
            for sub in subs:
                twisted = []
                for cols, (cos, sin) in zip((first, second), turns):
                    re = outer[stream, sub, of_freq(k), cols]
                    if k == 0:
                        twisted.append((re, jnp.zeros_like(re)))
                        continue
                    if k == blocks:
                        twisted.append((re * cos, -(re * sin)))
                        continue
                    im = outer[stream, sub, of_freq(k - 1, real_rows), cols]
                    twisted.append((re * cos + im * sin, im * cos - re * sin))
                (re_a, im_a), (re_b, im_b) = twisted
                halves[0].append(jnp.concatenate([re_a + re_b, im_a + im_b], axis=1))
                halves[1].append(jnp.concatenate([re_a - re_b, im_a - im_b], axis=1))
            at = slice(k * width, (k + 1) * width)
            for parts, high, low in (
                (halves[0], even_high, even_low),
                (halves[1], odd_high, odd_low),
            ):
                joined = jnp.concatenate(parts, axis=0)
                high[stream, at], low[stream, at] = split_parts(joined)

    outer_dft(0)
    outer_dft(1)
    twist(0)
    sig_even = inner_dft(even_high[0], even_low[0], even_ref)
    sig_odd = inner_dft(odd_high[0], odd_low[0], odd_ref)
    twist(1)
    ker_even = inner_dft(even_high[1], even_low[1], even_ref)
    ker_odd = inner_dft(odd_high[1], odd_low[1], odd_ref)
    for sig, ker, back_table_ref, out in (
        (sig_even, ker_even, even_ref, even),
        (sig_odd, ker_odd, back_ref, odd),
    ):
        sig_re, sig_im = sig[:, first], sig[:, second]
        ker_re, ker_im = ker[:, first], ker[:, second]
        prod_re = sig_re * ker_re - sig_im * ker_im
        prod_neg = -(sig_re * ker_im + sig_im * ker_re)
        product = jnp.concatenate([prod_re, prod_neg], axis=1)
        out[...] = inner_dft(*split_parts(product), back_table_ref)

    for k in range(blocks + 1):
        for cols, sign in ((first, 1), (second, -1)):
            cos, sin = cos_ref[k : k + 1, cols], sin_ref[k : k + 1, cols]
            for sub in subs:
                at = slice(k * width + sub * lines, k * width + (sub + 1) * lines)
                z = even[at] + odd[at] if sign > 0 else even[at] - odd[at]
                re, neg = z[:, first], z[:, second]
                outer[0, sub, of_freq(k), cols] = re * cos + neg * sin
                if 0 < k < blocks:
                    outer[0, sub, of_freq(k - 1, real_rows), cols] = re * sin - neg * cos
    parts = []
    for sub in subs:
        high, low = split_parts(outer[0, sub])
        back = jnp.dot(high_ref[...], low, preferred_element_type=F32)
        back += jnp.dot(low_ref[...], high, preferred_element_type=F32)
        back += jnp.dot(high_ref[...], high, preferred_element_type=F32)
        parts.append(back.reshape(blocks, lines, tok_rows))
    out_ref[...] = jnp.concatenate(parts, axis=1).astype(BF16)


def gate_kernel(order_in, order_out, q_ref, conv_ref, out_ref):
    groups, width, tok_rows = conv_ref.shape
    parts = [conv_ref[order_in.index(group)].astype(F32) for group in range(groups)]
    convolved = jnp.concatenate(parts, axis=0).T
    gated_rows = (q_ref[...].astype(F32) * convolved).astype(BF16)
    tokens = out_ref.shape[1]
    for n, group in enumerate(order_out):
        out_ref[n] = gated_rows[group * tokens : (group + 1) * tokens]


def norm_kernel(order, rows_ref, gain_ref, out_ref):
    groups, _, width = rows_ref.shape
    squares = 0.0
    for n in range(groups):
        widened = rows_ref[n].astype(F32)
        squares = squares + widened * widened
    total = jnp.sum(squares, axis=1, keepdims=True)
    scaling = lax.rsqrt(total / (groups * width) + 1e-05)
    for n, group in enumerate(order):
        cols = slice(group * width, (group + 1) * width)
        row = rows_ref[n].astype(F32)
        out_ref[:, cols] = (row * scaling * gain_ref[:, cols]).astype(BF16)


def on_device(kernel, out_shape, cost, scratch=(), **specs):
    return pl.pallas_call(
        kernel,
        out_shape=out_shape,
        scratch_shapes=list(scratch),
        compiler_params=pltpu.CompilerParams(vmem_limit_bytes=VMEM_BYTES),
        cost_estimate=pl.CostEstimate(
            flops=cost[0], bytes_accessed=cost[1], transcendentals=0
        ),
        **specs,
    )


def mix(k_stream, v_stream, filters, order):
    tok_rows, channels = k_stream.shape
    groups = len(order)
    shape = jax.ShapeDtypeStruct((groups, 2 * channels // groups, tok_rows), BF16)
    cost = (k_stream.size, 12 * k_stream.size)
    scratch = [pltpu.VMEM(k_stream.shape, BF16)] * 2
    scratch += [pltpu.VMEM(k_stream.shape, F32), pltpu.SemaphoreType.DMA((4,))]
    specs = [pl.BlockSpec(memory_space=pltpu.HBM)] * 3
    held = [
        pltpu.with_memory_space_constraint(array, pltpu.HBM)
        for array in (k_stream, v_stream, filters)
    ]
    kernel = functools.partial(mix_kernel, order)
    return on_device(kernel, shape, cost, scratch, in_specs=specs)(*held)


def convolve(pieces, order_in, order_out):
    blocks, rows, tok_rows = pieces.shape
    width = rows // 2
    lines = 8
    tables = (
        np.stack(twist_tables(blocks, tok_rows)),
        np.stack(inner_tables(tok_rows)),
        np.concatenate(
            outer_tables(blocks, tok_rows, lines, order_in, order_out), axis=0
        ),
    )
    shape = jax.ShapeDtypeStruct((blocks, width, tok_rows), BF16)
    freq_rows = (blocks + 1) * width
    scratch = [pltpu.VMEM((2, width // lines, 2 * blocks * lines, tok_rows), F32)]
    scratch += [pltpu.VMEM((2, freq_rows, tok_rows), BF16)] * 4
    scratch += [pltpu.VMEM((freq_rows, tok_rows), F32)] * 2
    cost = (2 * 3 * freq_rows * 3 * 2 * tok_rows * tok_rows, 2 * 2**20)
    return on_device(conv_kernel, shape, cost, scratch)(
        pieces, *(jnp.asarray(table) for table in tables)
    )


def gate(q_stream, convolved, order_in, order_out):
    tok_rows, channels = q_stream.shape
    count = len(order_out)
    shape = jax.ShapeDtypeStruct((count, tok_rows // count, channels), BF16)
    cost = (q_stream.size, 6 * q_stream.size)
    kernel = functools.partial(gate_kernel, order_in, order_out)
    return on_device(kernel, shape, cost)(q_stream, convolved)


def normalize(rows, norm_gain, order):
    groups, tokens, width = rows.shape
    channels = groups * width
    shape = jax.ShapeDtypeStruct((tokens, channels), BF16)
    cost = (6 * tokens * channels, 4 * tokens * channels + 4 * channels)
    kernel = functools.partial(norm_kernel, order)
    return on_device(kernel, shape, cost)(rows, norm_gain.reshape(1, channels))


def exchange(array, axis, order):
    return lax.all_to_all(
        array, axis, split_axis=0, concat_axis=0, axis_index_groups=[order], tiled=True
    )


def far_apart(count):
    far = [0]
    while len(far) < count:
        far = [2 * n for n in far] + [2 * n + 1 for n in far]
    return far


def listed(places):
    return places[::-1]


def local(q_stream, k_stream, v_stream, filters, norm_gain):
    ctx, ch = lax.axis_size("ctx"), lax.axis_size("ch")
    order_ctx = listed(
        [
            z * 4 + (x + n) % 2 * 2 + core
            for x in range(2)
            for n, z in enumerate(far_apart(ctx // 4))
            for core in range(2)
        ]
    )
    order_ch = listed([y * 2 + x for x in range(2) for y in far_apart(ch // 2)])
    pieces = exchange(mix(k_stream, v_stream, filters, order_ctx), "ctx", order_ctx)
    convolved = convolve(pieces, order_ctx, order_ctx)
    returned = exchange(convolved, "ctx", order_ctx)
    gated_rows = gate(q_stream, returned, order_ctx, order_ch)
    regrouped = exchange(gated_rows, "ch", order_ch)
    return normalize(regrouped, norm_gain, order_ch)


def solution(mesh):
    return jax.shard_map(
        local,
        mesh=mesh,
        in_specs=(P("ctx", "ch"), P("ctx", "ch"), P("ctx", "ch"), P("ctx", "ch"), P()),
        out_specs=P(("ctx", "ch"), None),
        check_vma=False,
    )
```

```python
import functools
import math

import jax
import jax.numpy as jnp
import numpy as np
from jax import lax
from jax.experimental import pallas as pl
from jax.experimental.pallas import tpu as pltpu
from jax.sharding import PartitionSpec as P

BF16 = jnp.bfloat16
F32 = jnp.float32
VMEM_BYTES = 40 * 2**20


def parts_of(table):
    high = table.astype(np.float32).astype(jnp.bfloat16)
    low = (table - high.astype(np.float64)).astype(np.float32).astype(jnp.bfloat16)
    return high, low


def stacked_table(matrix):
    table = np.block([[matrix.real, matrix.imag], [-matrix.imag, matrix.real]])
    high, low = parts_of(table)
    return np.concatenate([high, low], axis=0)


def inner_tables(tok_rows):
    half = np.arange(tok_rows // 2)
    even_turns = 2 * half[:, None] * half[None, :] % tok_rows
    odd_turns = half[:, None] * (2 * half[None, :] + 1) % tok_rows
    even, odd = (
        np.exp(-2j * np.pi * turns / tok_rows) for turns in (even_turns, odd_turns)
    )
    return stacked_table(even), stacked_table(odd), stacked_table(odd.T)


def outer_tables(blocks, tok_rows, lines, order_in, order_out):
    index = np.arange(blocks)
    freqs = np.arange(blocks + 1)
    angle = np.pi * (freqs[:, None] * index[None, :] % (2 * blocks)) / blocks
    forward = np.concatenate([np.cos(angle), -np.sin(angle)[1:blocks]], axis=0)
    weight = np.full((2 * blocks, 1), 2.0 / (2 * blocks * tok_rows))
    weight[0] *= 0.5
    weight[blocks] *= 0.5
    backward = (weight * forward).T
    apart = np.eye(lines)
    return (
        np.concatenate(parts_of(np.kron(forward[:, order_in], apart)), axis=1),
        *parts_of(np.kron(backward[order_out], apart)),
    )


def twist_tables(blocks, tok_rows):
    period = 2 * blocks * tok_rows
    index = np.arange(blocks + 1)[:, None] * np.arange(tok_rows)[None, :] % period
    angle = 2.0 * np.pi * index / period
    return np.cos(angle).astype(np.float32), np.sin(angle).astype(np.float32)


def mix_kernel(order, k_hbm, v_hbm, filters_hbm, out_ref, k_ref, v_ref, filters_ref, sems):
    groups, rows, tok_rows = out_ref.shape
    width = rows // 2
    half = tok_rows // 2
    halves = (slice(0, half), slice(half, tok_rows))
    pairs = [(k_hbm, k_ref), (v_hbm, v_ref)]
    pairs += [(filters_hbm.at[at], filters_ref.at[at]) for at in halves]
    copies = [
        pltpu.make_async_copy(source, target, sems.at[n])
        for n, (source, target) in enumerate(pairs)
    ]
    for copy in copies:
        copy.start()
    copies[0].wait()
    copies[1].wait()
    mixed = (k_ref[...].astype(F32) * v_ref[...].astype(F32)).T
    mixed = mixed.reshape(groups, width, tok_rows).astype(BF16)
    for n, group in enumerate(order):
        out_ref[n, :width] = mixed[group]
    for at, copy in zip(halves, copies[2:]):
        copy.wait()
        taps = filters_ref[at].T.reshape(groups, width, half).astype(BF16)
        for n, group in enumerate(order):
            out_ref[n, width:, at] = taps[group]


def split_parts(values):
    high = values.astype(BF16)
    return high, (values - high.astype(F32)).astype(BF16)


def inner_dft(high, low, table_ref):
    left = jnp.concatenate([high, low, high], axis=1)
    table = table_ref[...]
    right = jnp.concatenate([table[: high.shape[1]], table], axis=0)
    return jnp.dot(left, right, preferred_element_type=F32)


def conv_kernel(
    in_ref, twist_ref, inner_ref, outer_ref, out_ref,
    outer, even_high, even_low, odd_high, odd_low, even, odd,
):
    blocks, rows, tok_rows = in_ref.shape
    width = rows // 2
    half = tok_rows // 2
    first, second = slice(0, half), slice(half, tok_rows)
    lines = 8
    subs = range(width // lines)
    real_rows = (blocks + 1) * lines
    cos_ref, sin_ref = twist_ref.at[0], twist_ref.at[1]
    even_ref, odd_ref, back_ref = (inner_ref.at[n] for n in range(3))
    back_rows = blocks * lines
    high_ref = outer_ref.at[2 * back_rows : 3 * back_rows]
    low_ref = outer_ref.at[3 * back_rows : 4 * back_rows]

    def of_freq(k, start=0):
        return slice(start + k * lines, start + (k + 1) * lines)

    def outer_dft(stream):
        top = stream * width
        whole = in_ref[:, top : top + width].astype(F32)
        for sub in subs:
            data = whole[:, sub * lines : (sub + 1) * lines]
            data = data.reshape(blocks * lines, tok_rows).astype(BF16)
            outer[stream, sub] = jnp.dot(
                outer_ref[: 2 * back_rows],
                jnp.concatenate([data, data], axis=0),
                preferred_element_type=F32,
            )

    def twist(stream):
        for k in range(blocks + 1):
            halves = [[], []]
            turns = [(cos_ref[k : k + 1, at], sin_ref[k : k + 1, at]) for at in (first, second)]
            for sub in subs:
                twisted = []
                for cols, (cos, sin) in zip((first, second), turns):
                    re = outer[stream, sub, of_freq(k), cols]
                    if k == 0:
                        twisted.append((re, jnp.zeros_like(re)))
                        continue
                    if k == blocks:
                        twisted.append((re * cos, -(re * sin)))
                        continue
                    im = outer[stream, sub, of_freq(k - 1, real_rows), cols]
                    twisted.append((re * cos + im * sin, im * cos - re * sin))
                (re_a, im_a), (re_b, im_b) = twisted
                halves[0].append(jnp.concatenate([re_a + re_b, im_a + im_b], axis=1))
                halves[1].append(jnp.concatenate([re_a - re_b, im_a - im_b], axis=1))
            at = slice(k * width, (k + 1) * width)
            for parts, high, low in (
                (halves[0], even_high, even_low),
                (halves[1], odd_high, odd_low),
            ):
                joined = jnp.concatenate(parts, axis=0)
                high[stream, at], low[stream, at] = split_parts(joined)

    outer_dft(0)
    outer_dft(1)
    twist(0)
    sig_even = inner_dft(even_high[0], even_low[0], even_ref)
    sig_odd = inner_dft(odd_high[0], odd_low[0], odd_ref)
    twist(1)
    ker_even = inner_dft(even_high[1], even_low[1], even_ref)
    ker_odd = inner_dft(odd_high[1], odd_low[1], odd_ref)
    for sig, ker, back_table_ref, out in (
        (sig_even, ker_even, even_ref, even),
        (sig_odd, ker_odd, back_ref, odd),
    ):
        sig_re, sig_im = sig[:, first], sig[:, second]
        ker_re, ker_im = ker[:, first], ker[:, second]
        prod_re = sig_re * ker_re - sig_im * ker_im
        prod_neg = -(sig_re * ker_im + sig_im * ker_re)
        product = jnp.concatenate([prod_re, prod_neg], axis=1)
        out[...] = inner_dft(*split_parts(product), back_table_ref)

    for k in range(blocks + 1):
        for cols, sign in ((first, 1), (second, -1)):
            cos, sin = cos_ref[k : k + 1, cols], sin_ref[k : k + 1, cols]
            for sub in subs:
                at = slice(k * width + sub * lines, k * width + (sub + 1) * lines)
                z = even[at] + odd[at] if sign > 0 else even[at] - odd[at]
                re, neg = z[:, first], z[:, second]
                outer[0, sub, of_freq(k), cols] = re * cos + neg * sin
                if 0 < k < blocks:
                    outer[0, sub, of_freq(k - 1, real_rows), cols] = re * sin - neg * cos
    parts = []
    for sub in subs:
        high, low = split_parts(outer[0, sub])
        back = jnp.dot(high_ref[...], low, preferred_element_type=F32)
        back += jnp.dot(low_ref[...], high, preferred_element_type=F32)
        back += jnp.dot(high_ref[...], high, preferred_element_type=F32)
        parts.append(back.reshape(blocks, lines, tok_rows))
    out_ref[...] = jnp.concatenate(parts, axis=1).astype(BF16)


def gate_kernel(order_in, order_out, q_ref, conv_ref, out_ref):
    groups, width, tok_rows = conv_ref.shape
    parts = [conv_ref[order_in.index(group)].astype(F32) for group in range(groups)]
    convolved = jnp.concatenate(parts, axis=0).T
    gated_rows = (q_ref[...].astype(F32) * convolved).astype(BF16)
    tokens = out_ref.shape[1]
    for n, group in enumerate(order_out):
        out_ref[n] = gated_rows[group * tokens : (group + 1) * tokens]


def norm_kernel(order, rows_ref, gain_ref, out_ref):
    groups, _, width = rows_ref.shape
    squares = 0.0
    for n in range(groups):
        widened = rows_ref[n].astype(F32)
        squares = squares + widened * widened
    total = jnp.sum(squares, axis=1, keepdims=True)
    scaling = lax.rsqrt(total / (groups * width) + 1e-05)
    for n, group in enumerate(order):
        cols = slice(group * width, (group + 1) * width)
        row = rows_ref[n].astype(F32)
        out_ref[:, cols] = (row * scaling * gain_ref[:, cols]).astype(BF16)


def on_device(kernel, out_shape, cost, scratch=(), **specs):
    return pl.pallas_call(
        kernel,
        out_shape=out_shape,
        scratch_shapes=list(scratch),
        compiler_params=pltpu.CompilerParams(vmem_limit_bytes=VMEM_BYTES),
        cost_estimate=pl.CostEstimate(
            flops=cost[0], bytes_accessed=cost[1], transcendentals=0
        ),
        **specs,
    )


def mix(k_stream, v_stream, filters, order):
    tok_rows, channels = k_stream.shape
    groups = len(order)
    shape = jax.ShapeDtypeStruct((groups, 2 * channels // groups, tok_rows), BF16)
    cost = (k_stream.size, 12 * k_stream.size)
    scratch = [pltpu.VMEM(k_stream.shape, BF16)] * 2
    scratch += [pltpu.VMEM(k_stream.shape, F32), pltpu.SemaphoreType.DMA((4,))]
    specs = [pl.BlockSpec(memory_space=pltpu.HBM)] * 3
    held = [
        pltpu.with_memory_space_constraint(array, pltpu.HBM)
        for array in (k_stream, v_stream, filters)
    ]
    kernel = functools.partial(mix_kernel, order)
    return on_device(kernel, shape, cost, scratch, in_specs=specs)(*held)


def convolve(pieces, order_in, order_out):
    blocks, rows, tok_rows = pieces.shape
    width = rows // 2
    lines = 8
    tables = (
        np.stack(twist_tables(blocks, tok_rows)),
        np.stack(inner_tables(tok_rows)),
        np.concatenate(
            outer_tables(blocks, tok_rows, lines, order_in, order_out), axis=0
        ),
    )
    shape = jax.ShapeDtypeStruct((blocks, width, tok_rows), BF16)
    freq_rows = (blocks + 1) * width
    scratch = [pltpu.VMEM((2, width // lines, 2 * blocks * lines, tok_rows), F32)]
    scratch += [pltpu.VMEM((2, freq_rows, tok_rows), BF16)] * 4
    scratch += [pltpu.VMEM((freq_rows, tok_rows), F32)] * 2
    cost = (2 * 3 * freq_rows * 3 * 2 * tok_rows * tok_rows, 2 * 2**20)
    return on_device(conv_kernel, shape, cost, scratch)(
        pieces, *(jnp.asarray(table) for table in tables)
    )


def gate(q_stream, convolved, order_in, order_out):
    tok_rows, channels = q_stream.shape
    count = len(order_out)
    shape = jax.ShapeDtypeStruct((count, tok_rows // count, channels), BF16)
    cost = (q_stream.size, 6 * q_stream.size)
    kernel = functools.partial(gate_kernel, order_in, order_out)
    return on_device(kernel, shape, cost)(q_stream, convolved)


def normalize(rows, norm_gain, order):
    groups, tokens, width = rows.shape
    channels = groups * width
    shape = jax.ShapeDtypeStruct((tokens, channels), BF16)
    cost = (6 * tokens * channels, 4 * tokens * channels + 4 * channels)
    kernel = functools.partial(norm_kernel, order)
    return on_device(kernel, shape, cost)(rows, norm_gain.reshape(1, channels))


def exchange(array, axis, order):
    return lax.all_to_all(
        array, axis, split_axis=0, concat_axis=0, axis_index_groups=[order], tiled=True
    )


def far_apart(count):
    far = [0]
    while len(far) < count:
        far = [2 * n for n in far] + [2 * n + 1 for n in far]
    return far


def listed(places):
    return places[::-1]


def local(q_stream, k_stream, v_stream, filters, norm_gain):
    ctx, ch = lax.axis_size("ctx"), lax.axis_size("ch")
    order_in = listed(
        [
            z * 4 + (x + n) % 2 * 2 + core
            for x in range(2)
            for n, z in enumerate(far_apart(ctx // 4))
            for core in range(2)
        ]
    )
    order_back = listed(
        [
            z * 4 + (x + n) % 2 * 2 + core
            for core in range(2)
            for x in range(2)
            for n, z in enumerate(far_apart(ctx // 4))
        ]
    )
    order_ch = listed([y * 2 + x for x in range(2) for y in far_apart(ch // 2)])
    pieces = exchange(mix(k_stream, v_stream, filters, order_in), "ctx", order_in)
    convolved = convolve(pieces, order_in, order_back)
    returned = exchange(convolved, "ctx", order_back)
    gated_rows = gate(q_stream, returned, order_back, order_ch)
    regrouped = exchange(gated_rows, "ch", order_ch)
    return normalize(regrouped, norm_gain, order_ch)


def solution(mesh):
    return jax.shard_map(
        local,
        mesh=mesh,
        in_specs=(P("ctx", "ch"), P("ctx", "ch"), P("ctx", "ch"), P("ctx", "ch"), P()),
        out_specs=P(("ctx", "ch"), None),
        check_vma=False,
    )
```

```python
import functools
import math

import jax
import jax.numpy as jnp
import numpy as np
from jax import lax
from jax.experimental import pallas as pl
from jax.experimental.pallas import tpu as pltpu
from jax.sharding import PartitionSpec as P

BF16 = jnp.bfloat16
F32 = jnp.float32
VMEM_BYTES = 40 * 2**20


def parts_of(table):
    high = table.astype(np.float32).astype(jnp.bfloat16)
    low = (table - high.astype(np.float64)).astype(np.float32).astype(jnp.bfloat16)
    return high, low


def stacked_table(matrix):
    table = np.block([[matrix.real, matrix.imag], [-matrix.imag, matrix.real]])
    high, low = parts_of(table)
    return np.concatenate([high, low], axis=0)


def inner_tables(tok_rows):
    half = np.arange(tok_rows // 2)
    even_turns = 2 * half[:, None] * half[None, :] % tok_rows
    odd_turns = half[:, None] * (2 * half[None, :] + 1) % tok_rows
    even, odd = (
        np.exp(-2j * np.pi * turns / tok_rows) for turns in (even_turns, odd_turns)
    )
    return stacked_table(even), stacked_table(odd), stacked_table(odd.T)


def outer_tables(blocks, tok_rows, lines, order_in, order_out):
    index = np.arange(blocks)
    freqs = np.arange(blocks + 1)
    angle = np.pi * (freqs[:, None] * index[None, :] % (2 * blocks)) / blocks
    forward = np.concatenate([np.cos(angle), -np.sin(angle)[1:blocks]], axis=0)
    weight = np.full((2 * blocks, 1), 2.0 / (2 * blocks * tok_rows))
    weight[0] *= 0.5
    weight[blocks] *= 0.5
    backward = (weight * forward).T
    apart = np.eye(lines)
    return (
        np.concatenate(parts_of(np.kron(forward[:, order_in], apart)), axis=1),
        *parts_of(np.kron(backward[order_out], apart)),
    )


def twist_tables(blocks, tok_rows):
    period = 2 * blocks * tok_rows
    index = np.arange(blocks + 1)[:, None] * np.arange(tok_rows)[None, :] % period
    angle = 2.0 * np.pi * index / period
    return np.cos(angle).astype(np.float32), np.sin(angle).astype(np.float32)


def mix_kernel(order, k_hbm, v_hbm, filters_hbm, out_ref, k_ref, v_ref, filters_ref, sems):
    groups, rows, tok_rows = out_ref.shape
    width = rows // 2
    half = tok_rows // 2
    halves = (slice(0, half), slice(half, tok_rows))
    pairs = [(k_hbm, k_ref), (v_hbm, v_ref)]
    pairs += [(filters_hbm.at[at], filters_ref.at[at]) for at in halves]
    copies = [
        pltpu.make_async_copy(source, target, sems.at[n])
        for n, (source, target) in enumerate(pairs)
    ]
    for copy in copies:
        copy.start()
    copies[0].wait()
    copies[1].wait()
    mixed = (k_ref[...].astype(F32) * v_ref[...].astype(F32)).T
    mixed = mixed.reshape(groups, width, tok_rows).astype(BF16)
    for n, group in enumerate(order):
        out_ref[n, :width] = mixed[group]
    for at, copy in zip(halves, copies[2:]):
        copy.wait()
        taps = filters_ref[at].T.reshape(groups, width, half).astype(BF16)
        for n, group in enumerate(order):
            out_ref[n, width:, at] = taps[group]


def split_parts(values):
    high = values.astype(BF16)
    return high, (values - high.astype(F32)).astype(BF16)


def inner_dft(high, low, table_ref):
    left = jnp.concatenate([high, low, high], axis=1)
    table = table_ref[...]
    right = jnp.concatenate([table[: high.shape[1]], table], axis=0)
    return jnp.dot(left, right, preferred_element_type=F32)


def conv_kernel(
    in_ref, twist_ref, inner_ref, outer_ref, out_ref,
    outer, even_high, even_low, odd_high, odd_low, even, odd,
):
    blocks, rows, tok_rows = in_ref.shape
    width = rows // 2
    half = tok_rows // 2
    first, second = slice(0, half), slice(half, tok_rows)
    lines = 8
    subs = range(width // lines)
    real_rows = (blocks + 1) * lines
    cos_ref, sin_ref = twist_ref.at[0], twist_ref.at[1]
    even_ref, odd_ref, back_ref = (inner_ref.at[n] for n in range(3))
    back_rows = blocks * lines
    high_ref = outer_ref.at[2 * back_rows : 3 * back_rows]
    low_ref = outer_ref.at[3 * back_rows : 4 * back_rows]

    def of_freq(k, start=0):
        return slice(start + k * lines, start + (k + 1) * lines)

    def outer_dft(stream):
        top = stream * width
        whole = in_ref[:, top : top + width].astype(F32)
        for sub in subs:
            data = whole[:, sub * lines : (sub + 1) * lines]
            data = data.reshape(blocks * lines, tok_rows).astype(BF16)
            outer[stream, sub] = jnp.dot(
                outer_ref[: 2 * back_rows],
                jnp.concatenate([data, data], axis=0),
                preferred_element_type=F32,
            )

    def twist(stream):
        for k in range(blocks + 1):
            halves = [[], []]
            turns = [(cos_ref[k : k + 1, at], sin_ref[k : k + 1, at]) for at in (first, second)]
            for sub in subs:
                twisted = []
                for cols, (cos, sin) in zip((first, second), turns):
                    re = outer[stream, sub, of_freq(k), cols]
                    if k == 0:
                        twisted.append((re, jnp.zeros_like(re)))
                        continue
                    if k == blocks:
                        twisted.append((re * cos, -(re * sin)))
                        continue
                    im = outer[stream, sub, of_freq(k - 1, real_rows), cols]
                    twisted.append((re * cos + im * sin, im * cos - re * sin))
                (re_a, im_a), (re_b, im_b) = twisted
                halves[0].append(jnp.concatenate([re_a + re_b, im_a + im_b], axis=1))
                halves[1].append(jnp.concatenate([re_a - re_b, im_a - im_b], axis=1))
            at = slice(k * width, (k + 1) * width)
            for parts, high, low in (
                (halves[0], even_high, even_low),
                (halves[1], odd_high, odd_low),
            ):
                joined = jnp.concatenate(parts, axis=0)
                high[stream, at], low[stream, at] = split_parts(joined)

    outer_dft(0)
    outer_dft(1)
    twist(0)
    sig_even = inner_dft(even_high[0], even_low[0], even_ref)
    sig_odd = inner_dft(odd_high[0], odd_low[0], odd_ref)
    twist(1)
    ker_even = inner_dft(even_high[1], even_low[1], even_ref)
    ker_odd = inner_dft(odd_high[1], odd_low[1], odd_ref)
    for sig, ker, back_table_ref, out in (
        (sig_even, ker_even, even_ref, even),
        (sig_odd, ker_odd, back_ref, odd),
    ):
        sig_re, sig_im = sig[:, first], sig[:, second]
        ker_re, ker_im = ker[:, first], ker[:, second]
        prod_re = sig_re * ker_re - sig_im * ker_im
        prod_neg = -(sig_re * ker_im + sig_im * ker_re)
        product = jnp.concatenate([prod_re, prod_neg], axis=1)
        out[...] = inner_dft(*split_parts(product), back_table_ref)

    for k in range(blocks + 1):
        for cols, sign in ((first, 1), (second, -1)):
            cos, sin = cos_ref[k : k + 1, cols], sin_ref[k : k + 1, cols]
            for sub in subs:
                at = slice(k * width + sub * lines, k * width + (sub + 1) * lines)
                z = even[at] + odd[at] if sign > 0 else even[at] - odd[at]
                re, neg = z[:, first], z[:, second]
                outer[0, sub, of_freq(k), cols] = re * cos + neg * sin
                if 0 < k < blocks:
                    outer[0, sub, of_freq(k - 1, real_rows), cols] = re * sin - neg * cos
    parts = []
    for sub in subs:
        high, low = split_parts(outer[0, sub])
        back = jnp.dot(high_ref[...], low, preferred_element_type=F32)
        back += jnp.dot(low_ref[...], high, preferred_element_type=F32)
        back += jnp.dot(high_ref[...], high, preferred_element_type=F32)
        parts.append(back.reshape(blocks, lines, tok_rows))
    out_ref[...] = jnp.concatenate(parts, axis=1).astype(BF16)


def gate_kernel(order_in, order_out, q_ref, conv_ref, out_ref):
    groups, width, tok_rows = conv_ref.shape
    parts = [conv_ref[order_in.index(group)].astype(F32) for group in range(groups)]
    convolved = jnp.concatenate(parts, axis=0).T
    gated_rows = (q_ref[...].astype(F32) * convolved).astype(BF16)
    tokens = out_ref.shape[1]
    for n, group in enumerate(order_out):
        out_ref[n] = gated_rows[group * tokens : (group + 1) * tokens]


def norm_kernel(order, rows_ref, gain_ref, out_ref):
    groups, _, width = rows_ref.shape
    squares = 0.0
    for n in range(groups):
        widened = rows_ref[n].astype(F32)
        squares = squares + widened * widened
    total = jnp.sum(squares, axis=1, keepdims=True)
    scaling = lax.rsqrt(total / (groups * width) + 1e-05)
    for n, group in enumerate(order):
        cols = slice(group * width, (group + 1) * width)
        row = rows_ref[n].astype(F32)
        out_ref[:, cols] = (row * scaling * gain_ref[:, cols]).astype(BF16)


def on_device(kernel, out_shape, cost, scratch=(), **specs):
    return pl.pallas_call(
        kernel,
        out_shape=out_shape,
        scratch_shapes=list(scratch),
        compiler_params=pltpu.CompilerParams(vmem_limit_bytes=VMEM_BYTES),
        cost_estimate=pl.CostEstimate(
            flops=cost[0], bytes_accessed=cost[1], transcendentals=0
        ),
        **specs,
    )


def mix(k_stream, v_stream, filters, order):
    tok_rows, channels = k_stream.shape
    groups = len(order)
    shape = jax.ShapeDtypeStruct((groups, 2 * channels // groups, tok_rows), BF16)
    cost = (k_stream.size, 12 * k_stream.size)
    scratch = [pltpu.VMEM(k_stream.shape, BF16)] * 2
    scratch += [pltpu.VMEM(k_stream.shape, F32), pltpu.SemaphoreType.DMA((4,))]
    specs = [pl.BlockSpec(memory_space=pltpu.HBM)] * 3
    held = [
        pltpu.with_memory_space_constraint(array, pltpu.HBM)
        for array in (k_stream, v_stream, filters)
    ]
    kernel = functools.partial(mix_kernel, order)
    return on_device(kernel, shape, cost, scratch, in_specs=specs)(*held)


def convolve(pieces, order_in, order_out):
    blocks, rows, tok_rows = pieces.shape
    width = rows // 2
    lines = 8
    tables = (
        np.stack(twist_tables(blocks, tok_rows)),
        np.stack(inner_tables(tok_rows)),
        np.concatenate(
            outer_tables(blocks, tok_rows, lines, order_in, order_out), axis=0
        ),
    )
    shape = jax.ShapeDtypeStruct((blocks, width, tok_rows), BF16)
    freq_rows = (blocks + 1) * width
    scratch = [pltpu.VMEM((2, width // lines, 2 * blocks * lines, tok_rows), F32)]
    scratch += [pltpu.VMEM((2, freq_rows, tok_rows), BF16)] * 4
    scratch += [pltpu.VMEM((freq_rows, tok_rows), F32)] * 2
    cost = (2 * 3 * freq_rows * 3 * 2 * tok_rows * tok_rows, 2 * 2**20)
    return on_device(conv_kernel, shape, cost, scratch)(
        pieces, *(jnp.asarray(table) for table in tables)
    )


def gate(q_stream, convolved, order_in, order_out):
    tok_rows, channels = q_stream.shape
    count = len(order_out)
    shape = jax.ShapeDtypeStruct((count, tok_rows // count, channels), BF16)
    cost = (q_stream.size, 6 * q_stream.size)
    kernel = functools.partial(gate_kernel, order_in, order_out)
    return on_device(kernel, shape, cost)(q_stream, convolved)


def normalize(rows, norm_gain, order):
    groups, tokens, width = rows.shape
    channels = groups * width
    shape = jax.ShapeDtypeStruct((tokens, channels), BF16)
    cost = (6 * tokens * channels, 4 * tokens * channels + 4 * channels)
    kernel = functools.partial(norm_kernel, order)
    return on_device(kernel, shape, cost)(rows, norm_gain.reshape(1, channels))


def exchange(array, axis, order):
    return lax.all_to_all(
        array, axis, split_axis=0, concat_axis=0, axis_index_groups=[order], tiled=True
    )


def far_apart(count):
    far = [0]
    while len(far) < count:
        far = [2 * n for n in far] + [2 * n + 1 for n in far]
    return far


def listed(places):
    return places[::-1]


def local(q_stream, k_stream, v_stream, filters, norm_gain):
    ctx, ch = lax.axis_size("ctx"), lax.axis_size("ch")
    order_in = listed(
        [
            z * 4 + (x + z) % 2 * 2 + core
            for x in range(2)
            for z in range(ctx // 4)
            for core in range(2)
        ]
    )
    order_back = listed(
        [
            z * 4 + (x + n) % 2 * 2 + core
            for core in range(2)
            for x in range(2)
            for n, z in enumerate(far_apart(ctx // 4))
        ]
    )
    by_start = sorted(range(ch), key=lambda n: n // 2 + 4.6 * (n % 2))
    order_ch = listed(by_start)
    pieces = exchange(mix(k_stream, v_stream, filters, order_in), "ctx", order_in)
    convolved = convolve(pieces, order_in, order_back)
    returned = exchange(convolved, "ctx", order_back)
    gated_rows = gate(q_stream, returned, order_back, order_ch)
    regrouped = exchange(gated_rows, "ch", order_ch)
    return normalize(regrouped, norm_gain, order_ch)


def solution(mesh):
    return jax.shard_map(
        local,
        mesh=mesh,
        in_specs=(P("ctx", "ch"), P("ctx", "ch"), P("ctx", "ch"), P("ctx", "ch"), P()),
        out_specs=P(("ctx", "ch"), None),
        check_vma=False,
    )
```

```python
import functools
import math

import jax
import jax.numpy as jnp
import numpy as np
from jax import lax
from jax.experimental import pallas as pl
from jax.experimental.pallas import tpu as pltpu
from jax.sharding import PartitionSpec as P

BF16 = jnp.bfloat16
F32 = jnp.float32
VMEM_BYTES = 40 * 2**20


def parts_of(table):
    high = table.astype(np.float32).astype(jnp.bfloat16)
    low = (table - high.astype(np.float64)).astype(np.float32).astype(jnp.bfloat16)
    return high, low


def stacked_table(matrix):
    table = np.block([[matrix.real, matrix.imag], [-matrix.imag, matrix.real]])
    high, low = parts_of(table)
    return np.concatenate([high, low], axis=0)


def inner_tables(tok_rows):
    half = np.arange(tok_rows // 2)
    even_turns = 2 * half[:, None] * half[None, :] % tok_rows
    odd_turns = half[:, None] * (2 * half[None, :] + 1) % tok_rows
    even, odd = (
        np.exp(-2j * np.pi * turns / tok_rows) for turns in (even_turns, odd_turns)
    )
    return stacked_table(even), stacked_table(odd), stacked_table(odd.T)


def outer_tables(blocks, tok_rows, lines, order_in, order_out):
    index = np.arange(blocks)
    freqs = np.arange(blocks + 1)
    angle = np.pi * (freqs[:, None] * index[None, :] % (2 * blocks)) / blocks
    forward = np.concatenate([np.cos(angle), -np.sin(angle)[1:blocks]], axis=0)
    weight = np.full((2 * blocks, 1), 2.0 / (2 * blocks * tok_rows))
    weight[0] *= 0.5
    weight[blocks] *= 0.5
    backward = (weight * forward).T
    apart = np.eye(lines)
    return (
        np.concatenate(parts_of(np.kron(forward[:, order_in], apart)), axis=1),
        *parts_of(np.kron(backward[order_out], apart)),
    )


def twist_tables(blocks, tok_rows):
    period = 2 * blocks * tok_rows
    index = np.arange(blocks + 1)[:, None] * np.arange(tok_rows)[None, :] % period
    angle = 2.0 * np.pi * index / period
    return np.cos(angle).astype(np.float32), np.sin(angle).astype(np.float32)


def mix_kernel(order, k_hbm, v_hbm, filters_hbm, out_ref, k_ref, v_ref, filters_ref, sems):
    groups, rows, tok_rows = out_ref.shape
    width = rows // 2
    half = tok_rows // 2
    halves = (slice(0, half), slice(half, tok_rows))
    pairs = [(k_hbm, k_ref), (v_hbm, v_ref)]
    pairs += [(filters_hbm.at[at], filters_ref.at[at]) for at in halves]
    copies = [
        pltpu.make_async_copy(source, target, sems.at[n])
        for n, (source, target) in enumerate(pairs)
    ]
    for copy in copies:
        copy.start()
    copies[0].wait()
    copies[1].wait()
    mixed = (k_ref[...].astype(F32) * v_ref[...].astype(F32)).astype(BF16)
    mixed = mixed.T.reshape(groups, width, tok_rows)
    for n, group in enumerate(order):
        out_ref[n, :width] = mixed[group]
    for at, copy in zip(halves, copies[2:]):
        copy.wait()
        taps = filters_ref[at].astype(BF16).T.reshape(groups, width, half)
        for n, group in enumerate(order):
            out_ref[n, width:, at] = taps[group]


def split_parts(values):
    high = values.astype(BF16)
    return high, (values - high.astype(F32)).astype(BF16)


def inner_dft(high, low, table_ref):
    rows = high.shape[1]
    table_high, table_low = table_ref[:rows], table_ref[rows:]
    total = jnp.dot(high, table_low, preferred_element_type=F32)
    yield total
    total = total + jnp.dot(low, table_high, preferred_element_type=F32)
    yield total
    yield total + jnp.dot(high, table_high, preferred_element_type=F32)


def side_by_side(matmuls, others):
    steps = 3 * len(matmuls)
    done, results = 0, []
    for n, matmul in enumerate(matmuls):
        for m, result in enumerate(matmul):
            upto = len(others) * (3 * n + m + 1) // steps
            for other in others[done:upto]:
                other()
            done = upto
        results.append(result)
    return results


def conv_kernel(
    in_ref, twist_ref, inner_ref, outer_ref, out_ref,
    outer, even_high, even_low, odd_high, odd_low, even, odd,
):
    blocks, rows, tok_rows = in_ref.shape
    width = rows // 2
    half = tok_rows // 2
    first, second = slice(0, half), slice(half, tok_rows)
    lines = 8
    subs = range(width // lines)
    real_rows = (blocks + 1) * lines
    cos_ref, sin_ref = twist_ref.at[0], twist_ref.at[1]
    even_ref, odd_ref, back_ref = (inner_ref.at[n] for n in range(3))
    back_rows = blocks * lines
    high_ref = outer_ref.at[2 * back_rows : 3 * back_rows]
    low_ref = outer_ref.at[3 * back_rows : 4 * back_rows]

    def of_freq(k, start=0):
        return slice(start + k * lines, start + (k + 1) * lines)

    def outer_dft(stream):
        top = stream * width
        whole = in_ref[:, top : top + width].astype(F32)
        for sub in subs:
            data = whole[:, sub * lines : (sub + 1) * lines]
            data = data.reshape(blocks * lines, tok_rows).astype(BF16)
            outer[stream, sub] = jnp.dot(
                outer_ref[: 2 * back_rows],
                jnp.concatenate([data, data], axis=0),
                preferred_element_type=F32,
            )

    def twist(stream, k):
        halves = [[], []]
        turns = [(cos_ref[k : k + 1, at], sin_ref[k : k + 1, at]) for at in (first, second)]
        for sub in subs:
            twisted = []
            for cols, (cos, sin) in zip((first, second), turns):
                re = outer[stream, sub, of_freq(k), cols]
                if k == 0:
                    twisted.append((re, jnp.zeros_like(re)))
                    continue
                if k == blocks:
                    twisted.append((re * cos, -(re * sin)))
                    continue
                im = outer[stream, sub, of_freq(k - 1, real_rows), cols]
                twisted.append((re * cos + im * sin, im * cos - re * sin))
            (re_a, im_a), (re_b, im_b) = twisted
            halves[0].append(jnp.concatenate([re_a + re_b, im_a + im_b], axis=1))
            halves[1].append(jnp.concatenate([re_a - re_b, im_a - im_b], axis=1))
        at = slice(k * width, (k + 1) * width)
        for parts, high, low in (
            (halves[0], even_high, even_low),
            (halves[1], odd_high, odd_low),
        ):
            joined = jnp.concatenate(parts, axis=0)
            high[stream, at], low[stream, at] = split_parts(joined)

    def product(sig, ker):
        sig_re, sig_im = sig[:, first], sig[:, second]
        ker_re, ker_im = ker[:, first], ker[:, second]
        prod_re = sig_re * ker_re - sig_im * ker_im
        prod_neg = -(sig_re * ker_im + sig_im * ker_re)
        return split_parts(jnp.concatenate([prod_re, prod_neg], axis=1))

    outer_dft(0)
    outer_dft(1)
    for k in range(blocks + 1):
        twist(0, k)
    sig_even, sig_odd = side_by_side(
        [
            inner_dft(even_high[0], even_low[0], even_ref),
            inner_dft(odd_high[0], odd_low[0], odd_ref),
        ],
        [functools.partial(twist, 1, k) for k in range(blocks + 1)],
    )
    made = {}

    def make(name, sig, ker):
        made[name] = product(sig, ker)

    (ker_even,) = side_by_side([inner_dft(even_high[1], even_low[1], even_ref)], [])
    (ker_odd,) = side_by_side(
        [inner_dft(odd_high[1], odd_low[1], odd_ref)],
        [functools.partial(make, "even", sig_even, ker_even)],
    )
    (even[...],) = side_by_side(
        [inner_dft(*made["even"], even_ref)],
        [functools.partial(make, "odd", sig_odd, ker_odd)],
    )
    (odd[...],) = side_by_side([inner_dft(*made["odd"], back_ref)], [])

    for k in range(blocks + 1):
        for cols, sign in ((first, 1), (second, -1)):
            cos, sin = cos_ref[k : k + 1, cols], sin_ref[k : k + 1, cols]
            for sub in subs:
                at = slice(k * width + sub * lines, k * width + (sub + 1) * lines)
                z = even[at] + odd[at] if sign > 0 else even[at] - odd[at]
                re, neg = z[:, first], z[:, second]
                outer[0, sub, of_freq(k), cols] = re * cos + neg * sin
                if 0 < k < blocks:
                    outer[0, sub, of_freq(k - 1, real_rows), cols] = re * sin - neg * cos
    parts = []
    for sub in subs:
        high, low = split_parts(outer[0, sub])
        back = jnp.dot(high_ref[...], low, preferred_element_type=F32)
        back += jnp.dot(low_ref[...], high, preferred_element_type=F32)
        back += jnp.dot(high_ref[...], high, preferred_element_type=F32)
        parts.append(back.reshape(blocks, lines, tok_rows))
    out_ref[...] = jnp.concatenate(parts, axis=1).astype(BF16)


def gate_kernel(order_in, order_out, q_ref, conv_ref, out_ref):
    groups, width, tok_rows = conv_ref.shape
    parts = [conv_ref[order_in.index(group)] for group in range(groups)]
    convolved = jnp.concatenate(parts, axis=0).T.astype(F32)
    gated_rows = (q_ref[...].astype(F32) * convolved).astype(BF16)
    tokens = out_ref.shape[1]
    for n, group in enumerate(order_out):
        out_ref[n] = gated_rows[group * tokens : (group + 1) * tokens]


def norm_kernel(order, rows_ref, gain_ref, out_ref):
    groups, _, width = rows_ref.shape
    squares = 0.0
    for n in range(groups):
        widened = rows_ref[n].astype(F32)
        squares = squares + widened * widened
    total = jnp.sum(squares, axis=1, keepdims=True)
    scaling = lax.rsqrt(total / (groups * width) + 1e-05)
    for n, group in enumerate(order):
        cols = slice(group * width, (group + 1) * width)
        row = rows_ref[n].astype(F32)
        out_ref[:, cols] = (row * scaling * gain_ref[:, cols]).astype(BF16)


def on_device(kernel, out_shape, cost, scratch=(), **specs):
    return pl.pallas_call(
        kernel,
        out_shape=out_shape,
        scratch_shapes=list(scratch),
        compiler_params=pltpu.CompilerParams(vmem_limit_bytes=VMEM_BYTES),
        cost_estimate=pl.CostEstimate(
            flops=cost[0], bytes_accessed=cost[1], transcendentals=0
        ),
        **specs,
    )


def mix(k_stream, v_stream, filters, order):
    tok_rows, channels = k_stream.shape
    groups = len(order)
    shape = jax.ShapeDtypeStruct((groups, 2 * channels // groups, tok_rows), BF16)
    cost = (k_stream.size, 12 * k_stream.size)
    scratch = [pltpu.VMEM(k_stream.shape, BF16)] * 2
    scratch += [pltpu.VMEM(k_stream.shape, F32), pltpu.SemaphoreType.DMA((4,))]
    specs = [pl.BlockSpec(memory_space=pltpu.HBM)] * 3
    held = [
        pltpu.with_memory_space_constraint(array, pltpu.HBM)
        for array in (k_stream, v_stream, filters)
    ]
    kernel = functools.partial(mix_kernel, order)
    return on_device(kernel, shape, cost, scratch, in_specs=specs)(*held)


def convolve(pieces, order_in, order_out):
    blocks, rows, tok_rows = pieces.shape
    width = rows // 2
    lines = 8
    tables = (
        np.stack(twist_tables(blocks, tok_rows)),
        np.stack(inner_tables(tok_rows)),
        np.concatenate(
            outer_tables(blocks, tok_rows, lines, order_in, order_out), axis=0
        ),
    )
    shape = jax.ShapeDtypeStruct((blocks, width, tok_rows), BF16)
    freq_rows = (blocks + 1) * width
    scratch = [pltpu.VMEM((2, width // lines, 2 * blocks * lines, tok_rows), F32)]
    scratch += [pltpu.VMEM((2, freq_rows, tok_rows), BF16)] * 4
    scratch += [pltpu.VMEM((freq_rows, tok_rows), F32)] * 2
    cost = (2 * 3 * freq_rows * 3 * 2 * tok_rows * tok_rows, 2 * 2**20)
    return on_device(conv_kernel, shape, cost, scratch)(
        pieces, *(jnp.asarray(table) for table in tables)
    )


def gate(q_stream, convolved, order_in, order_out):
    tok_rows, channels = q_stream.shape
    count = len(order_out)
    shape = jax.ShapeDtypeStruct((count, tok_rows // count, channels), BF16)
    cost = (q_stream.size, 6 * q_stream.size)
    kernel = functools.partial(gate_kernel, order_in, order_out)
    return on_device(kernel, shape, cost)(q_stream, convolved)


def normalize(rows, norm_gain, order):
    groups, tokens, width = rows.shape
    channels = groups * width
    shape = jax.ShapeDtypeStruct((tokens, channels), BF16)
    cost = (6 * tokens * channels, 4 * tokens * channels + 4 * channels)
    kernel = functools.partial(norm_kernel, order)
    return on_device(kernel, shape, cost)(rows, norm_gain.reshape(1, channels))


def exchange(array, axis, order):
    return lax.all_to_all(
        array, axis, split_axis=0, concat_axis=0, axis_index_groups=[order], tiled=True
    )


def far_apart(count):
    far = [0]
    while len(far) < count:
        far = [2 * n for n in far] + [2 * n + 1 for n in far]
    return far


def listed(places):
    return places[::-1]


def local(q_stream, k_stream, v_stream, filters, norm_gain):
    ctx, ch = lax.axis_size("ctx"), lax.axis_size("ch")
    order_in = listed(
        [
            z * 4 + (x + n) % 2 * 2 + core
            for x in range(2)
            for n, z in enumerate(far_apart(ctx // 4))
            for core in range(2)
        ]
    )
    order_back = listed(
        [
            z * 4 + (x + n) % 2 * 2 + core
            for core in range(2)
            for x in range(2)
            for n, z in enumerate(far_apart(ctx // 4))
        ]
    )
    order_ch = listed([y * 2 + x for x in range(2) for y in far_apart(ch // 2)])
    pieces = exchange(mix(k_stream, v_stream, filters, order_in), "ctx", order_in)
    convolved = convolve(pieces, order_in, order_back)
    returned = exchange(convolved, "ctx", order_back)
    gated_rows = gate(q_stream, returned, order_back, order_ch)
    regrouped = exchange(gated_rows, "ch", order_ch)
    return normalize(regrouped, norm_gain, order_ch)


def solution(mesh):
    return jax.shard_map(
        local,
        mesh=mesh,
        in_specs=(P("ctx", "ch"), P("ctx", "ch"), P("ctx", "ch"), P("ctx", "ch"), P()),
        out_specs=P(("ctx", "ch"), None),
        check_vma=False,
    )
```

```python
import functools
import math

import jax
import jax.numpy as jnp
import numpy as np
from jax import lax
from jax.experimental import pallas as pl
from jax.experimental.pallas import tpu as pltpu
from jax.sharding import PartitionSpec as P

BF16 = jnp.bfloat16
F32 = jnp.float32
VMEM_BYTES = 40 * 2**20


def parts_of(table):
    high = table.astype(np.float32).astype(jnp.bfloat16)
    low = (table - high.astype(np.float64)).astype(np.float32).astype(jnp.bfloat16)
    return high, low


def stacked_table(matrix):
    table = np.block([[matrix.real, matrix.imag], [-matrix.imag, matrix.real]])
    high, low = parts_of(table)
    return np.concatenate([high, low], axis=0)


def inner_tables(tok_rows):
    half = np.arange(tok_rows // 2)
    even_turns = 2 * half[:, None] * half[None, :] % tok_rows
    odd_turns = half[:, None] * (2 * half[None, :] + 1) % tok_rows
    even, odd = (
        np.exp(-2j * np.pi * turns / tok_rows) for turns in (even_turns, odd_turns)
    )
    return stacked_table(even), stacked_table(odd), stacked_table(odd.T)


def outer_tables(blocks, tok_rows, lines, order_in, order_out):
    index = np.arange(blocks)
    freqs = np.arange(blocks + 1)
    angle = np.pi * (freqs[:, None] * index[None, :] % (2 * blocks)) / blocks
    forward = np.concatenate([np.cos(angle), -np.sin(angle)[1:blocks]], axis=0)
    weight = np.full((2 * blocks, 1), 2.0 / (2 * blocks * tok_rows))
    weight[0] *= 0.5
    weight[blocks] *= 0.5
    backward = (weight * forward).T
    apart = np.eye(lines)
    return (
        np.concatenate(parts_of(np.kron(forward[:, order_in], apart)), axis=1),
        *parts_of(np.kron(backward[order_out], apart)),
    )


def twist_tables(blocks, tok_rows):
    period = 2 * blocks * tok_rows
    index = np.arange(blocks + 1)[:, None] * np.arange(tok_rows)[None, :] % period
    angle = 2.0 * np.pi * index / period
    return np.cos(angle).astype(np.float32), np.sin(angle).astype(np.float32)


def mix_kernel(order, k_hbm, v_hbm, filters_hbm, out_ref, k_ref, v_ref, filters_ref, sems):
    groups, rows, tok_rows = out_ref.shape
    width = rows // 2
    half = tok_rows // 2
    halves = (slice(0, half), slice(half, tok_rows))
    pairs = [(k_hbm, k_ref), (v_hbm, v_ref)]
    pairs += [(filters_hbm.at[at], filters_ref.at[at]) for at in halves]
    copies = [
        pltpu.make_async_copy(source, target, sems.at[n])
        for n, (source, target) in enumerate(pairs)
    ]
    for copy in copies:
        copy.start()
    copies[0].wait()
    copies[1].wait()
    mixed = (k_ref[...].astype(F32) * v_ref[...].astype(F32)).astype(BF16)
    mixed = mixed.T.reshape(groups, width, tok_rows)
    for n, group in enumerate(order):
        out_ref[n, :width] = mixed[group]
    for at, copy in zip(halves, copies[2:]):
        copy.wait()
        taps = filters_ref[at].astype(BF16).T.reshape(groups, width, half)
        for n, group in enumerate(order):
            out_ref[n, width:, at] = taps[group]


def split_parts(values):
    high = values.astype(BF16)
    return high, (values - high.astype(F32)).astype(BF16)


def inner_dft(high, low, table_ref):
    rows = high.shape[1]
    table_high, table_low = table_ref[:rows], table_ref[rows:]
    total = jnp.dot(high, table_low, preferred_element_type=F32)
    yield total
    total = total + jnp.dot(low, table_high, preferred_element_type=F32)
    yield total
    yield total + jnp.dot(high, table_high, preferred_element_type=F32)


def side_by_side(matmuls, others):
    steps = 3 * len(matmuls)
    done, results = 0, []
    for n, matmul in enumerate(matmuls):
        for m, result in enumerate(matmul):
            upto = len(others) * (3 * n + m + 1) // steps
            for other in others[done:upto]:
                other()
            done = upto
        results.append(result)
    return results


def conv_kernel(
    in_ref, twist_ref, inner_ref, outer_ref, out_ref,
    outer, even_high, even_low, odd_high, odd_low, even, odd,
):
    blocks, rows, tok_rows = in_ref.shape
    width = rows // 2
    half = tok_rows // 2
    first, second = slice(0, half), slice(half, tok_rows)
    lines = 8
    subs = range(width // lines)
    real_rows = (blocks + 1) * lines
    cos_ref, sin_ref = twist_ref.at[0], twist_ref.at[1]
    even_ref, odd_ref, back_ref = (inner_ref.at[n] for n in range(3))
    back_rows = blocks * lines
    high_ref = outer_ref.at[2 * back_rows : 3 * back_rows]
    low_ref = outer_ref.at[3 * back_rows : 4 * back_rows]

    def of_freq(k, start=0):
        return slice(start + k * lines, start + (k + 1) * lines)

    def outer_dft(stream):
        top = stream * width
        whole = in_ref[:, top : top + width].astype(F32)
        for sub in subs:
            data = whole[:, sub * lines : (sub + 1) * lines]
            data = data.reshape(blocks * lines, tok_rows).astype(BF16)
            outer[stream, sub] = jnp.dot(
                outer_ref[: 2 * back_rows],
                jnp.concatenate([data, data], axis=0),
                preferred_element_type=F32,
            )

    def twist(stream, k):
        halves = [[], []]
        turns = [(cos_ref[k : k + 1, at], sin_ref[k : k + 1, at]) for at in (first, second)]
        for sub in subs:
            twisted = []
            for cols, (cos, sin) in zip((first, second), turns):
                re = outer[stream, sub, of_freq(k), cols]
                if k == 0:
                    twisted.append((re, jnp.zeros_like(re)))
                    continue
                if k == blocks:
                    twisted.append((re * cos, -(re * sin)))
                    continue
                im = outer[stream, sub, of_freq(k - 1, real_rows), cols]
                twisted.append((re * cos + im * sin, im * cos - re * sin))
            (re_a, im_a), (re_b, im_b) = twisted
            halves[0].append(jnp.concatenate([re_a + re_b, im_a + im_b], axis=1))
            halves[1].append(jnp.concatenate([re_a - re_b, im_a - im_b], axis=1))
        at = slice(k * width, (k + 1) * width)
        for parts, high, low in (
            (halves[0], even_high, even_low),
            (halves[1], odd_high, odd_low),
        ):
            joined = jnp.concatenate(parts, axis=0)
            high[stream, at], low[stream, at] = split_parts(joined)

    def product(sig, ker):
        sig_re, sig_im = sig[:, first], sig[:, second]
        ker_re, ker_im = ker[:, first], ker[:, second]
        prod_re = sig_re * ker_re - sig_im * ker_im
        prod_neg = -(sig_re * ker_im + sig_im * ker_re)
        return split_parts(jnp.concatenate([prod_re, prod_neg], axis=1))

    outer_dft(0)
    outer_dft(1)
    for k in range(blocks + 1):
        twist(0, k)
    sig_even, sig_odd = side_by_side(
        [
            inner_dft(even_high[0], even_low[0], even_ref),
            inner_dft(odd_high[0], odd_low[0], odd_ref),
        ],
        [functools.partial(twist, 1, k) for k in range(blocks + 1)],
    )
    made = {}

    def make(name, sig, ker):
        made[name] = product(sig, ker)

    (ker_even,) = side_by_side([inner_dft(even_high[1], even_low[1], even_ref)], [])
    (ker_odd,) = side_by_side(
        [inner_dft(odd_high[1], odd_low[1], odd_ref)],
        [functools.partial(make, "even", sig_even, ker_even)],
    )
    (even[...],) = side_by_side(
        [inner_dft(*made["even"], even_ref)],
        [functools.partial(make, "odd", sig_odd, ker_odd)],
    )
    (odd[...],) = side_by_side([inner_dft(*made["odd"], back_ref)], [])

    for k in range(blocks + 1):
        for cols, sign in ((first, 1), (second, -1)):
            cos, sin = cos_ref[k : k + 1, cols], sin_ref[k : k + 1, cols]
            for sub in subs:
                at = slice(k * width + sub * lines, k * width + (sub + 1) * lines)
                z = even[at] + odd[at] if sign > 0 else even[at] - odd[at]
                re, neg = z[:, first], z[:, second]
                outer[0, sub, of_freq(k), cols] = re * cos + neg * sin
                if 0 < k < blocks:
                    outer[0, sub, of_freq(k - 1, real_rows), cols] = re * sin - neg * cos
    parts = []
    for sub in subs:
        high, low = split_parts(outer[0, sub])
        back = jnp.dot(high_ref[...], low, preferred_element_type=F32)
        back += jnp.dot(low_ref[...], high, preferred_element_type=F32)
        back += jnp.dot(high_ref[...], high, preferred_element_type=F32)
        parts.append(back.reshape(blocks, lines, tok_rows))
    out_ref[...] = jnp.concatenate(parts, axis=1).astype(BF16)


def gate_kernel(order_in, order_out, q_ref, conv_ref, out_ref):
    groups, width, tok_rows = conv_ref.shape
    parts = [conv_ref[order_in.index(group)] for group in range(groups)]
    convolved = jnp.concatenate(parts, axis=0).T.astype(F32)
    gated_rows = (q_ref[...].astype(F32) * convolved).astype(BF16)
    tokens = out_ref.shape[1]
    for n, group in enumerate(order_out):
        out_ref[n] = gated_rows[group * tokens : (group + 1) * tokens]


def norm_kernel(order, rows_ref, gain_ref, out_ref):
    groups, _, width = rows_ref.shape
    squares = 0.0
    for n in range(groups):
        widened = rows_ref[n].astype(F32)
        squares = squares + widened * widened
    total = jnp.sum(squares, axis=1, keepdims=True)
    scaling = lax.rsqrt(total / (groups * width) + 1e-05)
    for n, group in enumerate(order):
        cols = slice(group * width, (group + 1) * width)
        row = rows_ref[n].astype(F32)
        out_ref[:, cols] = (row * scaling * gain_ref[:, cols]).astype(BF16)


def on_device(kernel, out_shape, cost, scratch=(), **specs):
    return pl.pallas_call(
        kernel,
        out_shape=out_shape,
        scratch_shapes=list(scratch),
        compiler_params=pltpu.CompilerParams(vmem_limit_bytes=VMEM_BYTES),
        cost_estimate=pl.CostEstimate(
            flops=cost[0], bytes_accessed=cost[1], transcendentals=0
        ),
        **specs,
    )


def mix(k_stream, v_stream, filters, order):
    tok_rows, channels = k_stream.shape
    groups = len(order)
    shape = jax.ShapeDtypeStruct((groups, 2 * channels // groups, tok_rows), BF16)
    cost = (k_stream.size, 12 * k_stream.size)
    scratch = [pltpu.VMEM(k_stream.shape, BF16)] * 2
    scratch += [pltpu.VMEM(k_stream.shape, F32), pltpu.SemaphoreType.DMA((4,))]
    specs = [pl.BlockSpec(memory_space=pltpu.HBM)] * 3
    held = [
        pltpu.with_memory_space_constraint(array, pltpu.HBM)
        for array in (k_stream, v_stream, filters)
    ]
    kernel = functools.partial(mix_kernel, order)
    return on_device(kernel, shape, cost, scratch, in_specs=specs)(*held)


def convolve(pieces, order_in, order_out):
    blocks, rows, tok_rows = pieces.shape
    width = rows // 2
    lines = 8
    tables = (
        np.stack(twist_tables(blocks, tok_rows)),
        np.stack(inner_tables(tok_rows)),
        np.concatenate(
            outer_tables(blocks, tok_rows, lines, order_in, order_out), axis=0
        ),
    )
    shape = jax.ShapeDtypeStruct((blocks, width, tok_rows), BF16)
    freq_rows = (blocks + 1) * width
    scratch = [pltpu.VMEM((2, width // lines, 2 * blocks * lines, tok_rows), F32)]
    scratch += [pltpu.VMEM((2, freq_rows, tok_rows), BF16)] * 4
    scratch += [pltpu.VMEM((freq_rows, tok_rows), F32)] * 2
    cost = (2 * 3 * freq_rows * 3 * 2 * tok_rows * tok_rows, 2 * 2**20)
    return on_device(conv_kernel, shape, cost, scratch)(
        pieces, *(jnp.asarray(table) for table in tables)
    )


def gate(q_stream, convolved, order_in, order_out):
    tok_rows, channels = q_stream.shape
    count = len(order_out)
    shape = jax.ShapeDtypeStruct((count, tok_rows // count, channels), BF16)
    cost = (q_stream.size, 6 * q_stream.size)
    kernel = functools.partial(gate_kernel, order_in, order_out)
    return on_device(kernel, shape, cost)(q_stream, convolved)


def normalize(rows, norm_gain, order):
    groups, tokens, width = rows.shape
    channels = groups * width
    shape = jax.ShapeDtypeStruct((tokens, channels), BF16)
    cost = (6 * tokens * channels, 4 * tokens * channels + 4 * channels)
    kernel = functools.partial(norm_kernel, order)
    return on_device(kernel, shape, cost)(rows, norm_gain.reshape(1, channels))


def exchange(array, axis, order):
    return lax.all_to_all(
        array, axis, split_axis=0, concat_axis=0, axis_index_groups=[order], tiled=True
    )


def far_apart(count):
    return [(n + 1) // 2 if n % 2 else -n // 2 % count for n in range(count)]


def listed(places):
    return places[::-1]


def local(q_stream, k_stream, v_stream, filters, norm_gain):
    ctx, ch = lax.axis_size("ctx"), lax.axis_size("ch")
    order_in = listed(
        [
            z * 4 + (x + n) % 2 * 2 + core
            for x in range(2)
            for n, z in enumerate(far_apart(ctx // 4))
            for core in range(2)
        ]
    )
    order_back = listed(
        [
            z * 4 + (x + n) % 2 * 2 + core
            for core in range(2)
            for x in range(2)
            for n, z in enumerate(far_apart(ctx // 4))
        ]
    )
    order_ch = listed([y * 2 + x for x in range(2) for y in far_apart(ch // 2)])
    pieces = exchange(mix(k_stream, v_stream, filters, order_in), "ctx", order_in)
    convolved = convolve(pieces, order_in, order_back)
    returned = exchange(convolved, "ctx", order_back)
    gated_rows = gate(q_stream, returned, order_back, order_ch)
    regrouped = exchange(gated_rows, "ch", order_ch)
    return normalize(regrouped, norm_gain, order_ch)


def solution(mesh):
    return jax.shard_map(
        local,
        mesh=mesh,
        in_specs=(P("ctx", "ch"), P("ctx", "ch"), P("ctx", "ch"), P("ctx", "ch"), P()),
        out_specs=P(("ctx", "ch"), None),
        check_vma=False,
    )
```

```python
import functools
import math

import jax
import jax.numpy as jnp
import numpy as np
from jax import lax
from jax.experimental import pallas as pl
from jax.experimental.pallas import tpu as pltpu
from jax.sharding import PartitionSpec as P

BF16 = jnp.bfloat16
F32 = jnp.float32
VMEM_BYTES = 40 * 2**20


def parts_of(table):
    high = table.astype(np.float32).astype(jnp.bfloat16)
    low = (table - high.astype(np.float64)).astype(np.float32).astype(jnp.bfloat16)
    return high, low


def stacked_table(matrix):
    table = np.block([[matrix.real, matrix.imag], [-matrix.imag, matrix.real]])
    high, low = parts_of(table)
    return np.concatenate([high, low], axis=0)


def inner_tables(tok_rows):
    half = np.arange(tok_rows // 2)
    even_turns = 2 * half[:, None] * half[None, :] % tok_rows
    odd_turns = half[:, None] * (2 * half[None, :] + 1) % tok_rows
    even, odd = (
        np.exp(-2j * np.pi * turns / tok_rows) for turns in (even_turns, odd_turns)
    )
    return stacked_table(even), stacked_table(odd), stacked_table(odd.T)


def outer_tables(blocks, tok_rows, lines, order_in, order_out):
    index = np.arange(blocks)
    freqs = np.arange(blocks + 1)
    angle = np.pi * (freqs[:, None] * index[None, :] % (2 * blocks)) / blocks
    forward = np.concatenate([np.cos(angle), -np.sin(angle)[1:blocks]], axis=0)
    weight = np.full((2 * blocks, 1), 2.0 / (2 * blocks * tok_rows))
    weight[0] *= 0.5
    weight[blocks] *= 0.5
    backward = (weight * forward).T
    apart = np.eye(lines)
    return (
        np.concatenate(parts_of(np.kron(forward[:, order_in], apart)), axis=1),
        *parts_of(np.kron(backward[order_out], apart)),
    )


def twist_tables(blocks, tok_rows):
    period = 2 * blocks * tok_rows
    index = np.arange(blocks + 1)[:, None] * np.arange(tok_rows)[None, :] % period
    angle = 2.0 * np.pi * index / period
    return np.cos(angle).astype(np.float32), np.sin(angle).astype(np.float32)


def mix_kernel(order, k_hbm, v_hbm, filters_hbm, out_ref, k_ref, v_ref, filters_ref, sems):
    groups, rows, tok_rows = out_ref.shape
    width = rows // 2
    half = tok_rows // 2
    halves = (slice(0, half), slice(half, tok_rows))
    pairs = [(k_hbm, k_ref), (v_hbm, v_ref)]
    pairs += [(filters_hbm.at[at], filters_ref.at[at]) for at in halves]
    copies = [
        pltpu.make_async_copy(source, target, sems.at[n])
        for n, (source, target) in enumerate(pairs)
    ]
    for copy in copies:
        copy.start()
    copies[0].wait()
    copies[1].wait()
    mixed = (k_ref[...].astype(F32) * v_ref[...].astype(F32)).astype(BF16)
    mixed = mixed.T.reshape(groups, width, tok_rows)
    for n, group in enumerate(order):
        out_ref[n, :width] = mixed[group]
    for at, copy in zip(halves, copies[2:]):
        copy.wait()
        taps = filters_ref[at].astype(BF16).T.reshape(groups, width, half)
        for n, group in enumerate(order):
            out_ref[n, width:, at] = taps[group]


def split_parts(values):
    high = values.astype(BF16)
    return high, (values - high.astype(F32)).astype(BF16)


def inner_dft(high, low, table_ref):
    rows = high.shape[1]
    table_high, table_low = table_ref[:rows], table_ref[rows:]
    total = jnp.dot(high, table_low, preferred_element_type=F32)
    yield total
    total = total + jnp.dot(low, table_high, preferred_element_type=F32)
    yield total
    yield total + jnp.dot(high, table_high, preferred_element_type=F32)


def side_by_side(matmuls, others):
    steps = 3 * len(matmuls)
    done, results = 0, []
    for n, matmul in enumerate(matmuls):
        for m, result in enumerate(matmul):
            upto = len(others) * (3 * n + m + 1) // steps
            for other in others[done:upto]:
                other()
            done = upto
        results.append(result)
    return results


def conv_kernel(
    in_ref, twist_ref, inner_ref, outer_ref, out_ref,
    outer, even_high, even_low, odd_high, odd_low, even, odd,
):
    blocks, rows, tok_rows = in_ref.shape
    width = rows // 2
    half = tok_rows // 2
    first, second = slice(0, half), slice(half, tok_rows)
    lines = 8
    subs = range(width // lines)
    real_rows = (blocks + 1) * lines
    cos_ref, sin_ref = twist_ref.at[0], twist_ref.at[1]
    even_ref, odd_ref, back_ref = (inner_ref.at[n] for n in range(3))
    back_rows = blocks * lines
    high_ref = outer_ref.at[2 * back_rows : 3 * back_rows]
    low_ref = outer_ref.at[3 * back_rows : 4 * back_rows]

    def of_freq(k, start=0):
        return slice(start + k * lines, start + (k + 1) * lines)

    def outer_dft(stream):
        top = stream * width
        whole = in_ref[:, top : top + width].astype(F32)
        for sub in subs:
            data = whole[:, sub * lines : (sub + 1) * lines]
            data = data.reshape(blocks * lines, tok_rows).astype(BF16)
            outer[stream, sub] = jnp.dot(
                outer_ref[: 2 * back_rows],
                jnp.concatenate([data, data], axis=0),
                preferred_element_type=F32,
            )

    def twist(stream, k):
        halves = [[], []]
        turns = [(cos_ref[k : k + 1, at], sin_ref[k : k + 1, at]) for at in (first, second)]
        for sub in subs:
            twisted = []
            for cols, (cos, sin) in zip((first, second), turns):
                re = outer[stream, sub, of_freq(k), cols]
                if k == 0:
                    twisted.append((re, jnp.zeros_like(re)))
                    continue
                if k == blocks:
                    twisted.append((re * cos, -(re * sin)))
                    continue
                im = outer[stream, sub, of_freq(k - 1, real_rows), cols]
                twisted.append((re * cos + im * sin, im * cos - re * sin))
            (re_a, im_a), (re_b, im_b) = twisted
            halves[0].append(jnp.concatenate([re_a + re_b, im_a + im_b], axis=1))
            halves[1].append(jnp.concatenate([re_a - re_b, im_a - im_b], axis=1))
        at = slice(k * width, (k + 1) * width)
        for parts, high, low in (
            (halves[0], even_high, even_low),
            (halves[1], odd_high, odd_low),
        ):
            joined = jnp.concatenate(parts, axis=0)
            high[stream, at], low[stream, at] = split_parts(joined)

    def product(sig, ker):
        sig_re, sig_im = sig[:, first], sig[:, second]
        ker_re, ker_im = ker[:, first], ker[:, second]
        prod_re = sig_re * ker_re - sig_im * ker_im
        prod_neg = -(sig_re * ker_im + sig_im * ker_re)
        return split_parts(jnp.concatenate([prod_re, prod_neg], axis=1))

    outer_dft(0)
    outer_dft(1)
    for k in range(blocks + 1):
        twist(0, k)
    sig_even, sig_odd = side_by_side(
        [
            inner_dft(even_high[0], even_low[0], even_ref),
            inner_dft(odd_high[0], odd_low[0], odd_ref),
        ],
        [functools.partial(twist, 1, k) for k in range(blocks + 1)],
    )
    made = {}

    def make(name, sig, ker):
        made[name] = product(sig, ker)

    (ker_even,) = side_by_side([inner_dft(even_high[1], even_low[1], even_ref)], [])
    (ker_odd,) = side_by_side(
        [inner_dft(odd_high[1], odd_low[1], odd_ref)],
        [functools.partial(make, "even", sig_even, ker_even)],
    )
    (even[...],) = side_by_side(
        [inner_dft(*made["even"], even_ref)],
        [functools.partial(make, "odd", sig_odd, ker_odd)],
    )
    (odd[...],) = side_by_side([inner_dft(*made["odd"], back_ref)], [])

    for k in range(blocks + 1):
        for cols, sign in ((first, 1), (second, -1)):
            cos, sin = cos_ref[k : k + 1, cols], sin_ref[k : k + 1, cols]
            for sub in subs:
                at = slice(k * width + sub * lines, k * width + (sub + 1) * lines)
                z = even[at] + odd[at] if sign > 0 else even[at] - odd[at]
                re, neg = z[:, first], z[:, second]
                outer[0, sub, of_freq(k), cols] = re * cos + neg * sin
                if 0 < k < blocks:
                    outer[0, sub, of_freq(k - 1, real_rows), cols] = re * sin - neg * cos
    parts = []
    for sub in subs:
        high, low = split_parts(outer[0, sub])
        back = jnp.dot(high_ref[...], low, preferred_element_type=F32)
        back += jnp.dot(low_ref[...], high, preferred_element_type=F32)
        back += jnp.dot(high_ref[...], high, preferred_element_type=F32)
        parts.append(back.reshape(blocks, lines, tok_rows))
    out_ref[...] = jnp.concatenate(parts, axis=1).astype(BF16)


def gate_kernel(order_in, order_out, q_ref, conv_ref, out_ref):
    groups, width, tok_rows = conv_ref.shape
    parts = [conv_ref[order_in.index(group)] for group in range(groups)]
    convolved = jnp.concatenate(parts, axis=0).T.astype(F32)
    gated_rows = (q_ref[...].astype(F32) * convolved).astype(BF16)
    tokens = out_ref.shape[1]
    for n, group in enumerate(order_out):
        out_ref[n] = gated_rows[group * tokens : (group + 1) * tokens]


def norm_kernel(order, rows_ref, gain_ref, out_ref):
    groups, _, width = rows_ref.shape
    squares = 0.0
    for n in range(groups):
        widened = rows_ref[n].astype(F32)
        squares = squares + widened * widened
    total = jnp.sum(squares, axis=1, keepdims=True)
    scaling = lax.rsqrt(total / (groups * width) + 1e-05)
    for n, group in enumerate(order):
        cols = slice(group * width, (group + 1) * width)
        row = rows_ref[n].astype(F32)
        out_ref[:, cols] = (row * scaling * gain_ref[:, cols]).astype(BF16)


def on_device(kernel, out_shape, cost, scratch=(), **specs):
    return pl.pallas_call(
        kernel,
        out_shape=out_shape,
        scratch_shapes=list(scratch),
        compiler_params=pltpu.CompilerParams(vmem_limit_bytes=VMEM_BYTES),
        cost_estimate=pl.CostEstimate(
            flops=cost[0], bytes_accessed=cost[1], transcendentals=0
        ),
        **specs,
    )


def mix(k_stream, v_stream, filters, order):
    tok_rows, channels = k_stream.shape
    groups = len(order)
    shape = jax.ShapeDtypeStruct((groups, 2 * channels // groups, tok_rows), BF16)
    cost = (k_stream.size, 12 * k_stream.size)
    scratch = [pltpu.VMEM(k_stream.shape, BF16)] * 2
    scratch += [pltpu.VMEM(k_stream.shape, F32), pltpu.SemaphoreType.DMA((4,))]
    specs = [pl.BlockSpec(memory_space=pltpu.HBM)] * 3
    held = [
        pltpu.with_memory_space_constraint(array, pltpu.HBM)
        for array in (k_stream, v_stream, filters)
    ]
    kernel = functools.partial(mix_kernel, order)
    return on_device(kernel, shape, cost, scratch, in_specs=specs)(*held)


def convolve(pieces, order_in, order_out):
    blocks, rows, tok_rows = pieces.shape
    width = rows // 2
    lines = 8
    tables = (
        np.stack(twist_tables(blocks, tok_rows)),
        np.stack(inner_tables(tok_rows)),
        np.concatenate(
            outer_tables(blocks, tok_rows, lines, order_in, order_out), axis=0
        ),
    )
    shape = jax.ShapeDtypeStruct((blocks, width, tok_rows), BF16)
    freq_rows = (blocks + 1) * width
    scratch = [pltpu.VMEM((2, width // lines, 2 * blocks * lines, tok_rows), F32)]
    scratch += [pltpu.VMEM((2, freq_rows, tok_rows), BF16)] * 4
    scratch += [pltpu.VMEM((freq_rows, tok_rows), F32)] * 2
    cost = (2 * 3 * freq_rows * 3 * 2 * tok_rows * tok_rows, 2 * 2**20)
    return on_device(conv_kernel, shape, cost, scratch)(
        pieces, *(jnp.asarray(table) for table in tables)
    )


def gate(q_stream, convolved, order_in, order_out):
    tok_rows, channels = q_stream.shape
    count = len(order_out)
    shape = jax.ShapeDtypeStruct((count, tok_rows // count, channels), BF16)
    cost = (q_stream.size, 6 * q_stream.size)
    kernel = functools.partial(gate_kernel, order_in, order_out)
    return on_device(kernel, shape, cost)(q_stream, convolved)


def normalize(rows, norm_gain, order):
    groups, tokens, width = rows.shape
    channels = groups * width
    shape = jax.ShapeDtypeStruct((tokens, channels), BF16)
    cost = (6 * tokens * channels, 4 * tokens * channels + 4 * channels)
    kernel = functools.partial(norm_kernel, order)
    return on_device(kernel, shape, cost)(rows, norm_gain.reshape(1, channels))


def exchange(array, axis, order):
    return lax.all_to_all(
        array, axis, split_axis=0, concat_axis=0, axis_index_groups=[order], tiled=True
    )


def far_apart(count):
    far = [0]
    while len(far) < count:
        far = [2 * n for n in far] + [2 * n + 1 for n in far]
    return far


def opposite(count):
    return [n // 2 + n % 2 * (count // 2) for n in range(count)]


def strided(count, step):
    return [n * step % count for n in range(count)]


def listed(places):
    return places[::-1]


def local(q_stream, k_stream, v_stream, filters, norm_gain):
    ctx, ch = lax.axis_size("ctx"), lax.axis_size("ch")
    order_in = listed(
        [
            z * 4 + (x + n) % 2 * 2 + core
            for x in range(2)
            for n, z in enumerate(opposite(ctx // 4))
            for core in range(2)
        ]
    )
    order_back = listed(
        [
            z * 4 + (x + n) % 2 * 2 + core
            for core in range(2)
            for x in range(2)
            for n, z in enumerate(strided(ctx // 4, 3))
        ]
    )
    order_ch = listed([y * 2 + x for x in range(2) for y in far_apart(ch // 2)])
    pieces = exchange(mix(k_stream, v_stream, filters, order_in), "ctx", order_in)
    convolved = convolve(pieces, order_in, order_back)
    returned = exchange(convolved, "ctx", order_back)
    gated_rows = gate(q_stream, returned, order_back, order_ch)
    regrouped = exchange(gated_rows, "ch", order_ch)
    return normalize(regrouped, norm_gain, order_ch)


def solution(mesh):
    return jax.shard_map(
        local,
        mesh=mesh,
        in_specs=(P("ctx", "ch"), P("ctx", "ch"), P("ctx", "ch"), P("ctx", "ch"), P()),
        out_specs=P(("ctx", "ch"), None),
        check_vma=False,
    )
```

```python
import functools
import math

import jax
import jax.numpy as jnp
import numpy as np
from jax import lax
from jax.experimental import pallas as pl
from jax.experimental.pallas import tpu as pltpu
from jax.sharding import PartitionSpec as P

BF16 = jnp.bfloat16
F32 = jnp.float32
VMEM_BYTES = 40 * 2**20


def parts_of(table):
    high = table.astype(np.float32).astype(jnp.bfloat16)
    low = (table - high.astype(np.float64)).astype(np.float32).astype(jnp.bfloat16)
    return high, low


def stacked_table(matrix):
    table = np.block([[matrix.real, matrix.imag], [-matrix.imag, matrix.real]])
    high, low = parts_of(table)
    return np.concatenate([high, low], axis=0)


def inner_tables(tok_rows):
    half = np.arange(tok_rows // 2)
    even_turns = 2 * half[:, None] * half[None, :] % tok_rows
    odd_turns = half[:, None] * (2 * half[None, :] + 1) % tok_rows
    even, odd = (
        np.exp(-2j * np.pi * turns / tok_rows) for turns in (even_turns, odd_turns)
    )
    return stacked_table(even), stacked_table(odd), stacked_table(odd.T)


def outer_tables(blocks, tok_rows, lines, order_in, order_out):
    index = np.arange(blocks)
    freqs = np.arange(blocks + 1)
    angle = np.pi * (freqs[:, None] * index[None, :] % (2 * blocks)) / blocks
    forward = np.concatenate([np.cos(angle), -np.sin(angle)[1:blocks]], axis=0)
    weight = np.full((2 * blocks, 1), 2.0 / (2 * blocks * tok_rows))
    weight[0] *= 0.5
    weight[blocks] *= 0.5
    backward = (weight * forward).T
    apart = np.eye(lines)
    return (
        np.concatenate(parts_of(np.kron(forward[:, order_in], apart)), axis=1),
        *parts_of(np.kron(backward[order_out], apart)),
    )


def twist_tables(blocks, tok_rows):
    period = 2 * blocks * tok_rows
    index = np.arange(blocks + 1)[:, None] * np.arange(tok_rows)[None, :] % period
    angle = 2.0 * np.pi * index / period
    return np.cos(angle).astype(np.float32), np.sin(angle).astype(np.float32)


def mix_kernel(order, k_hbm, v_hbm, filters_hbm, out_ref, k_ref, v_ref, filters_ref, sems):
    groups, rows, tok_rows = out_ref.shape
    width = rows // 2
    half = tok_rows // 2
    halves = (slice(0, half), slice(half, tok_rows))
    pairs = [(k_hbm, k_ref), (v_hbm, v_ref)]
    pairs += [(filters_hbm.at[at], filters_ref.at[at]) for at in halves]
    copies = [
        pltpu.make_async_copy(source, target, sems.at[n])
        for n, (source, target) in enumerate(pairs)
    ]
    for copy in copies:
        copy.start()
    copies[0].wait()
    copies[1].wait()
    mixed = (k_ref[...].astype(F32) * v_ref[...].astype(F32)).astype(BF16)
    mixed = mixed.T.reshape(groups, width, tok_rows)
    for n, group in enumerate(order):
        out_ref[n, :width] = mixed[group]
    for at, copy in zip(halves, copies[2:]):
        copy.wait()
        taps = filters_ref[at].astype(BF16).T.reshape(groups, width, half)
        for n, group in enumerate(order):
            out_ref[n, width:, at] = taps[group]


def split_parts(values):
    high = values.astype(BF16)
    return high, (values - high.astype(F32)).astype(BF16)


def inner_dft(high, low, table_ref):
    rows = high.shape[1]
    table_high, table_low = table_ref[:rows], table_ref[rows:]
    total = jnp.dot(high, table_low, preferred_element_type=F32)
    yield total
    total = total + jnp.dot(low, table_high, preferred_element_type=F32)
    yield total
    yield total + jnp.dot(high, table_high, preferred_element_type=F32)


def side_by_side(matmuls, others):
    steps = 3 * len(matmuls)
    done, results = 0, []
    for n, matmul in enumerate(matmuls):
        for m, result in enumerate(matmul):
            upto = len(others) * (3 * n + m + 1) // steps
            for other in others[done:upto]:
                other()
            done = upto
        results.append(result)
    return results


def conv_kernel(
    in_ref, twist_ref, inner_ref, outer_ref, out_ref,
    outer, even_high, even_low, odd_high, odd_low, even, odd,
):
    blocks, rows, tok_rows = in_ref.shape
    width = rows // 2
    half = tok_rows // 2
    first, second = slice(0, half), slice(half, tok_rows)
    lines = 8
    subs = range(width // lines)
    real_rows = (blocks + 1) * lines
    cos_ref, sin_ref = twist_ref.at[0], twist_ref.at[1]
    even_ref, odd_ref, back_ref = (inner_ref.at[n] for n in range(3))
    back_rows = blocks * lines
    high_ref = outer_ref.at[2 * back_rows : 3 * back_rows]
    low_ref = outer_ref.at[3 * back_rows : 4 * back_rows]

    def of_freq(k, start=0):
        return slice(start + k * lines, start + (k + 1) * lines)

    def outer_dft(stream):
        top = stream * width
        whole = in_ref[:, top : top + width].astype(F32)
        for sub in subs:
            data = whole[:, sub * lines : (sub + 1) * lines]
            data = data.reshape(blocks * lines, tok_rows).astype(BF16)
            outer[stream, sub] = jnp.dot(
                outer_ref[: 2 * back_rows],
                jnp.concatenate([data, data], axis=0),
                preferred_element_type=F32,
            )

    def twist(stream, k):
        halves = [[], []]
        turns = [(cos_ref[k : k + 1, at], sin_ref[k : k + 1, at]) for at in (first, second)]
        for sub in subs:
            twisted = []
            for cols, (cos, sin) in zip((first, second), turns):
                re = outer[stream, sub, of_freq(k), cols]
                if k == 0:
                    twisted.append((re, jnp.zeros_like(re)))
                    continue
                if k == blocks:
                    twisted.append((re * cos, -(re * sin)))
                    continue
                im = outer[stream, sub, of_freq(k - 1, real_rows), cols]
                twisted.append((re * cos + im * sin, im * cos - re * sin))
            (re_a, im_a), (re_b, im_b) = twisted
            halves[0].append(jnp.concatenate([re_a + re_b, im_a + im_b], axis=1))
            halves[1].append(jnp.concatenate([re_a - re_b, im_a - im_b], axis=1))
        at = slice(k * width, (k + 1) * width)
        for parts, high, low in (
            (halves[0], even_high, even_low),
            (halves[1], odd_high, odd_low),
        ):
            joined = jnp.concatenate(parts, axis=0)
            high[stream, at], low[stream, at] = split_parts(joined)

    def product(sig, ker):
        sig_re, sig_im = sig[:, first], sig[:, second]
        ker_re, ker_im = ker[:, first], ker[:, second]
        prod_re = sig_re * ker_re - sig_im * ker_im
        prod_neg = -(sig_re * ker_im + sig_im * ker_re)
        return split_parts(jnp.concatenate([prod_re, prod_neg], axis=1))

    outer_dft(0)
    outer_dft(1)
    for k in range(blocks + 1):
        twist(0, k)
    sig_even, sig_odd = side_by_side(
        [
            inner_dft(even_high[0], even_low[0], even_ref),
            inner_dft(odd_high[0], odd_low[0], odd_ref),
        ],
        [functools.partial(twist, 1, k) for k in range(blocks + 1)],
    )
    made = {}

    def make(name, sig, ker):
        made[name] = product(sig, ker)

    (ker_even,) = side_by_side([inner_dft(even_high[1], even_low[1], even_ref)], [])
    (ker_odd,) = side_by_side(
        [inner_dft(odd_high[1], odd_low[1], odd_ref)],
        [functools.partial(make, "even", sig_even, ker_even)],
    )
    (even[...],) = side_by_side(
        [inner_dft(*made["even"], even_ref)],
        [functools.partial(make, "odd", sig_odd, ker_odd)],
    )
    (odd[...],) = side_by_side([inner_dft(*made["odd"], back_ref)], [])

    for k in range(blocks + 1):
        for cols, sign in ((first, 1), (second, -1)):
            cos, sin = cos_ref[k : k + 1, cols], sin_ref[k : k + 1, cols]
            for sub in subs:
                at = slice(k * width + sub * lines, k * width + (sub + 1) * lines)
                z = even[at] + odd[at] if sign > 0 else even[at] - odd[at]
                re, neg = z[:, first], z[:, second]
                outer[0, sub, of_freq(k), cols] = re * cos + neg * sin
                if 0 < k < blocks:
                    outer[0, sub, of_freq(k - 1, real_rows), cols] = re * sin - neg * cos
    parts = []
    for sub in subs:
        high, low = split_parts(outer[0, sub])
        back = jnp.dot(high_ref[...], low, preferred_element_type=F32)
        back += jnp.dot(low_ref[...], high, preferred_element_type=F32)
        back += jnp.dot(high_ref[...], high, preferred_element_type=F32)
        parts.append(back.reshape(blocks, lines, tok_rows))
    out_ref[...] = jnp.concatenate(parts, axis=1).astype(BF16)


def gate_kernel(order_in, order_out, q_ref, conv_ref, out_ref):
    groups, width, tok_rows = conv_ref.shape
    parts = [conv_ref[order_in.index(group)] for group in range(groups)]
    convolved = jnp.concatenate(parts, axis=0).T.astype(F32)
    gated_rows = (q_ref[...].astype(F32) * convolved).astype(BF16)
    tokens = out_ref.shape[1]
    for n, group in enumerate(order_out):
        out_ref[n] = gated_rows[group * tokens : (group + 1) * tokens]


def norm_kernel(order, rows_ref, gain_ref, out_ref):
    groups, _, width = rows_ref.shape
    squares = 0.0
    for n in range(groups):
        widened = rows_ref[n].astype(F32)
        squares = squares + widened * widened
    total = jnp.sum(squares, axis=1, keepdims=True)
    scaling = lax.rsqrt(total / (groups * width) + 1e-05)
    for n, group in enumerate(order):
        cols = slice(group * width, (group + 1) * width)
        row = rows_ref[n].astype(F32)
        out_ref[:, cols] = (row * scaling * gain_ref[:, cols]).astype(BF16)


def on_device(kernel, out_shape, cost, scratch=(), **specs):
    return pl.pallas_call(
        kernel,
        out_shape=out_shape,
        scratch_shapes=list(scratch),
        compiler_params=pltpu.CompilerParams(vmem_limit_bytes=VMEM_BYTES),
        cost_estimate=pl.CostEstimate(
            flops=cost[0], bytes_accessed=cost[1], transcendentals=0
        ),
        **specs,
    )


def mix(k_stream, v_stream, filters, order):
    tok_rows, channels = k_stream.shape
    groups = len(order)
    shape = jax.ShapeDtypeStruct((groups, 2 * channels // groups, tok_rows), BF16)
    cost = (k_stream.size, 12 * k_stream.size)
    scratch = [pltpu.VMEM(k_stream.shape, BF16)] * 2
    scratch += [pltpu.VMEM(k_stream.shape, F32), pltpu.SemaphoreType.DMA((4,))]
    specs = [pl.BlockSpec(memory_space=pltpu.HBM)] * 3
    held = [
        pltpu.with_memory_space_constraint(array, pltpu.HBM)
        for array in (k_stream, v_stream, filters)
    ]
    kernel = functools.partial(mix_kernel, order)
    return on_device(kernel, shape, cost, scratch, in_specs=specs)(*held)


def convolve(pieces, order_in, order_out):
    blocks, rows, tok_rows = pieces.shape
    width = rows // 2
    lines = 8
    tables = (
        np.stack(twist_tables(blocks, tok_rows)),
        np.stack(inner_tables(tok_rows)),
        np.concatenate(
            outer_tables(blocks, tok_rows, lines, order_in, order_out), axis=0
        ),
    )
    shape = jax.ShapeDtypeStruct((blocks, width, tok_rows), BF16)
    freq_rows = (blocks + 1) * width
    scratch = [pltpu.VMEM((2, width // lines, 2 * blocks * lines, tok_rows), F32)]
    scratch += [pltpu.VMEM((2, freq_rows, tok_rows), BF16)] * 4
    scratch += [pltpu.VMEM((freq_rows, tok_rows), F32)] * 2
    cost = (2 * 3 * freq_rows * 3 * 2 * tok_rows * tok_rows, 2 * 2**20)
    return on_device(conv_kernel, shape, cost, scratch)(
        pieces, *(jnp.asarray(table) for table in tables)
    )


def gate(q_stream, convolved, order_in, order_out):
    tok_rows, channels = q_stream.shape
    count = len(order_out)
    shape = jax.ShapeDtypeStruct((count, tok_rows // count, channels), BF16)
    cost = (q_stream.size, 6 * q_stream.size)
    kernel = functools.partial(gate_kernel, order_in, order_out)
    return on_device(kernel, shape, cost)(q_stream, convolved)


def normalize(rows, norm_gain, order):
    groups, tokens, width = rows.shape
    channels = groups * width
    shape = jax.ShapeDtypeStruct((tokens, channels), BF16)
    cost = (6 * tokens * channels, 4 * tokens * channels + 4 * channels)
    kernel = functools.partial(norm_kernel, order)
    return on_device(kernel, shape, cost)(rows, norm_gain.reshape(1, channels))


def exchange(array, axis, order):
    return lax.all_to_all(
        array, axis, split_axis=0, concat_axis=0, axis_index_groups=[order], tiled=True
    )


def far_apart(count):
    far = [0]
    while len(far) < count:
        far = [2 * n for n in far] + [2 * n + 1 for n in far]
    return far


def opposite(count):
    return [n // 2 + n % 2 * (count // 2) for n in range(count)]


def listed(places):
    return places[::-1]


def local(q_stream, k_stream, v_stream, filters, norm_gain):
    ctx, ch = lax.axis_size("ctx"), lax.axis_size("ch")
    order_in = listed(
        [
            z * 4 + (x + n) % 2 * 2 + core
            for x in range(2)
            for n, z in enumerate(opposite(ctx // 4))
            for core in range(2)
        ]
    )
    order_back = listed(
        [
            z * 4 + (x + n) % 2 * 2 + core
            for core in range(2)
            for x in range(2)
            for n, z in enumerate(opposite(ctx // 4))
        ]
    )
    order_ch = listed([y * 2 + x for x in range(2) for y in far_apart(ch // 2)])
    pieces = exchange(mix(k_stream, v_stream, filters, order_in), "ctx", order_in)
    convolved = convolve(pieces, order_in, order_back)
    returned = exchange(convolved, "ctx", order_back)
    gated_rows = gate(q_stream, returned, order_back, order_ch)
    regrouped = exchange(gated_rows, "ch", order_ch)
    return normalize(regrouped, norm_gain, order_ch)


def solution(mesh):
    return jax.shard_map(
        local,
        mesh=mesh,
        in_specs=(P("ctx", "ch"), P("ctx", "ch"), P("ctx", "ch"), P("ctx", "ch"), P()),
        out_specs=P(("ctx", "ch"), None),
        check_vma=False,
    )
```

```python
import functools
import math

import jax
import jax.numpy as jnp
import numpy as np
from jax import lax
from jax.experimental import pallas as pl
from jax.experimental.pallas import tpu as pltpu
from jax.sharding import PartitionSpec as P

BF16 = jnp.bfloat16
F32 = jnp.float32
VMEM_BYTES = 40 * 2**20


def parts_of(table):
    high = table.astype(np.float32).astype(jnp.bfloat16)
    low = (table - high.astype(np.float64)).astype(np.float32).astype(jnp.bfloat16)
    return high, low


def stacked_table(matrix):
    table = np.block([[matrix.real, matrix.imag], [-matrix.imag, matrix.real]])
    high, low = parts_of(table)
    return np.concatenate([high, low], axis=0)


def inner_tables(tok_rows):
    half = np.arange(tok_rows // 2)
    even_turns = 2 * half[:, None] * half[None, :] % tok_rows
    odd_turns = half[:, None] * (2 * half[None, :] + 1) % tok_rows
    even, odd = (
        np.exp(-2j * np.pi * turns / tok_rows) for turns in (even_turns, odd_turns)
    )
    return stacked_table(even), stacked_table(odd), stacked_table(odd.T)


def outer_tables(blocks, tok_rows, lines, order_in, order_out):
    index = np.arange(blocks)
    freqs = np.arange(blocks + 1)
    angle = np.pi * (freqs[:, None] * index[None, :] % (2 * blocks)) / blocks
    forward = np.concatenate([np.cos(angle), -np.sin(angle)[1:blocks]], axis=0)
    weight = np.full((2 * blocks, 1), 2.0 / (2 * blocks * tok_rows))
    weight[0] *= 0.5
    weight[blocks] *= 0.5
    backward = (weight * forward).T
    apart = np.eye(lines)
    return (
        np.concatenate(parts_of(np.kron(forward[:, order_in], apart)), axis=1),
        *parts_of(np.kron(backward[order_out], apart)),
    )


def twist_tables(blocks, tok_rows):
    period = 2 * blocks * tok_rows
    index = np.arange(blocks + 1)[:, None] * np.arange(tok_rows)[None, :] % period
    angle = 2.0 * np.pi * index / period
    return np.cos(angle).astype(np.float32), np.sin(angle).astype(np.float32)


def mix_kernel(order, k_hbm, v_hbm, filters_hbm, out_ref, k_ref, v_ref, filters_ref, sems):
    groups, rows, tok_rows = out_ref.shape
    width = rows // 2
    half = tok_rows // 2
    halves = (slice(0, half), slice(half, tok_rows))
    pairs = [(k_hbm, k_ref), (v_hbm, v_ref)]
    pairs += [(filters_hbm.at[at], filters_ref.at[at]) for at in halves]
    copies = [
        pltpu.make_async_copy(source, target, sems.at[n])
        for n, (source, target) in enumerate(pairs)
    ]
    for copy in copies:
        copy.start()
    copies[0].wait()
    copies[1].wait()
    mixed = (k_ref[...].astype(F32) * v_ref[...].astype(F32)).astype(BF16)
    mixed = mixed.T.reshape(groups, width, tok_rows)
    for n, group in enumerate(order):
        out_ref[n, :width] = mixed[group]
    for at, copy in zip(halves, copies[2:]):
        copy.wait()
        taps = filters_ref[at].astype(BF16).T.reshape(groups, width, half)
        for n, group in enumerate(order):
            out_ref[n, width:, at] = taps[group]


def split_parts(values):
    high = values.astype(BF16)
    return high, (values - high.astype(F32)).astype(BF16)


def inner_dft(high, low, table_ref):
    rows = high.shape[1]
    table_high, table_low = table_ref[:rows], table_ref[rows:]
    total = jnp.dot(high, table_low, preferred_element_type=F32)
    yield total
    total = total + jnp.dot(low, table_high, preferred_element_type=F32)
    yield total
    yield total + jnp.dot(high, table_high, preferred_element_type=F32)


def side_by_side(matmuls, others):
    steps = 3 * len(matmuls)
    done, results = 0, []
    for n, matmul in enumerate(matmuls):
        for m, result in enumerate(matmul):
            upto = len(others) * (3 * n + m + 1) // steps
            for other in others[done:upto]:
                other()
            done = upto
        results.append(result)
    return results


def conv_kernel(
    in_ref, twist_ref, inner_ref, outer_ref, out_ref,
    outer, even_high, even_low, odd_high, odd_low, even, odd,
):
    blocks, rows, tok_rows = in_ref.shape
    width = rows // 2
    half = tok_rows // 2
    first, second = slice(0, half), slice(half, tok_rows)
    lines = 8
    subs = range(width // lines)
    real_rows = (blocks + 1) * lines
    cos_ref, sin_ref = twist_ref.at[0], twist_ref.at[1]
    even_ref, odd_ref, back_ref = (inner_ref.at[n] for n in range(3))
    back_rows = blocks * lines
    high_ref = outer_ref.at[2 * back_rows : 3 * back_rows]
    low_ref = outer_ref.at[3 * back_rows : 4 * back_rows]

    def of_freq(k, start=0):
        return slice(start + k * lines, start + (k + 1) * lines)

    def outer_dft(stream):
        top = stream * width
        whole = in_ref[:, top : top + width].astype(F32)
        for sub in subs:
            data = whole[:, sub * lines : (sub + 1) * lines]
            data = data.reshape(blocks * lines, tok_rows).astype(BF16)
            outer[stream, sub] = jnp.dot(
                outer_ref[: 2 * back_rows],
                jnp.concatenate([data, data], axis=0),
                preferred_element_type=F32,
            )

    def twist(stream, k):
        halves = [[], []]
        turns = [(cos_ref[k : k + 1, at], sin_ref[k : k + 1, at]) for at in (first, second)]
        for sub in subs:
            twisted = []
            for cols, (cos, sin) in zip((first, second), turns):
                re = outer[stream, sub, of_freq(k), cols]
                if k == 0:
                    twisted.append((re, jnp.zeros_like(re)))
                    continue
                if k == blocks:
                    twisted.append((re * cos, -(re * sin)))
                    continue
                im = outer[stream, sub, of_freq(k - 1, real_rows), cols]
                twisted.append((re * cos + im * sin, im * cos - re * sin))
            (re_a, im_a), (re_b, im_b) = twisted
            halves[0].append(jnp.concatenate([re_a + re_b, im_a + im_b], axis=1))
            halves[1].append(jnp.concatenate([re_a - re_b, im_a - im_b], axis=1))
        at = slice(k * width, (k + 1) * width)
        for parts, high, low in (
            (halves[0], even_high, even_low),
            (halves[1], odd_high, odd_low),
        ):
            joined = jnp.concatenate(parts, axis=0)
            high[stream, at], low[stream, at] = split_parts(joined)

    def product(sig, ker):
        sig_re, sig_im = sig[:, first], sig[:, second]
        ker_re, ker_im = ker[:, first], ker[:, second]
        prod_re = sig_re * ker_re - sig_im * ker_im
        prod_neg = -(sig_re * ker_im + sig_im * ker_re)
        return split_parts(jnp.concatenate([prod_re, prod_neg], axis=1))

    outer_dft(0)
    outer_dft(1)
    for k in range(blocks + 1):
        twist(0, k)
    sig_even, sig_odd = side_by_side(
        [
            inner_dft(even_high[0], even_low[0], even_ref),
            inner_dft(odd_high[0], odd_low[0], odd_ref),
        ],
        [functools.partial(twist, 1, k) for k in range(blocks + 1)],
    )
    made = {}

    def make(name, sig, ker):
        made[name] = product(sig, ker)

    (ker_even,) = side_by_side([inner_dft(even_high[1], even_low[1], even_ref)], [])
    (ker_odd,) = side_by_side(
        [inner_dft(odd_high[1], odd_low[1], odd_ref)],
        [functools.partial(make, "even", sig_even, ker_even)],
    )
    (even[...],) = side_by_side(
        [inner_dft(*made["even"], even_ref)],
        [functools.partial(make, "odd", sig_odd, ker_odd)],
    )
    (odd[...],) = side_by_side([inner_dft(*made["odd"], back_ref)], [])

    for k in range(blocks + 1):
        for cols, sign in ((first, 1), (second, -1)):
            cos, sin = cos_ref[k : k + 1, cols], sin_ref[k : k + 1, cols]
            for sub in subs:
                at = slice(k * width + sub * lines, k * width + (sub + 1) * lines)
                z = even[at] + odd[at] if sign > 0 else even[at] - odd[at]
                re, neg = z[:, first], z[:, second]
                outer[0, sub, of_freq(k), cols] = re * cos + neg * sin
                if 0 < k < blocks:
                    outer[0, sub, of_freq(k - 1, real_rows), cols] = re * sin - neg * cos
    parts = []
    for sub in subs:
        high, low = split_parts(outer[0, sub])
        back = jnp.dot(high_ref[...], low, preferred_element_type=F32)
        back += jnp.dot(low_ref[...], high, preferred_element_type=F32)
        back += jnp.dot(high_ref[...], high, preferred_element_type=F32)
        parts.append(back.reshape(blocks, lines, tok_rows))
    out_ref[...] = jnp.concatenate(parts, axis=1).astype(BF16)


def gate_kernel(order_in, order_out, q_ref, conv_ref, out_ref):
    groups, width, tok_rows = conv_ref.shape
    parts = [conv_ref[order_in.index(group)] for group in range(groups)]
    convolved = jnp.concatenate(parts, axis=0).T.astype(F32)
    gated_rows = (q_ref[...].astype(F32) * convolved).astype(BF16)
    tokens = out_ref.shape[1]
    for n, group in enumerate(order_out):
        out_ref[n] = gated_rows[group * tokens : (group + 1) * tokens]


def norm_kernel(order, rows_ref, gain_ref, out_ref):
    groups, _, width = rows_ref.shape
    squares = 0.0
    for n in range(groups):
        widened = rows_ref[n].astype(F32)
        squares = squares + widened * widened
    total = jnp.sum(squares, axis=1, keepdims=True)
    scaling = lax.rsqrt(total / (groups * width) + 1e-05)
    for n, group in enumerate(order):
        cols = slice(group * width, (group + 1) * width)
        row = rows_ref[n].astype(F32)
        out_ref[:, cols] = (row * scaling * gain_ref[:, cols]).astype(BF16)


def on_device(kernel, out_shape, cost, scratch=(), **specs):
    return pl.pallas_call(
        kernel,
        out_shape=out_shape,
        scratch_shapes=list(scratch),
        compiler_params=pltpu.CompilerParams(vmem_limit_bytes=VMEM_BYTES),
        cost_estimate=pl.CostEstimate(
            flops=cost[0], bytes_accessed=cost[1], transcendentals=0
        ),
        **specs,
    )


def mix(k_stream, v_stream, filters, order):
    tok_rows, channels = k_stream.shape
    groups = len(order)
    shape = jax.ShapeDtypeStruct((groups, 2 * channels // groups, tok_rows), BF16)
    cost = (k_stream.size, 12 * k_stream.size)
    scratch = [pltpu.VMEM(k_stream.shape, BF16)] * 2
    scratch += [pltpu.VMEM(k_stream.shape, F32), pltpu.SemaphoreType.DMA((4,))]
    specs = [pl.BlockSpec(memory_space=pltpu.HBM)] * 3
    held = [
        pltpu.with_memory_space_constraint(array, pltpu.HBM)
        for array in (k_stream, v_stream, filters)
    ]
    kernel = functools.partial(mix_kernel, order)
    return on_device(kernel, shape, cost, scratch, in_specs=specs)(*held)


def convolve(pieces, order_in, order_out):
    blocks, rows, tok_rows = pieces.shape
    width = rows // 2
    lines = 8
    tables = (
        np.stack(twist_tables(blocks, tok_rows)),
        np.stack(inner_tables(tok_rows)),
        np.concatenate(
            outer_tables(blocks, tok_rows, lines, order_in, order_out), axis=0
        ),
    )
    shape = jax.ShapeDtypeStruct((blocks, width, tok_rows), BF16)
    freq_rows = (blocks + 1) * width
    scratch = [pltpu.VMEM((2, width // lines, 2 * blocks * lines, tok_rows), F32)]
    scratch += [pltpu.VMEM((2, freq_rows, tok_rows), BF16)] * 4
    scratch += [pltpu.VMEM((freq_rows, tok_rows), F32)] * 2
    cost = (2 * 3 * freq_rows * 3 * 2 * tok_rows * tok_rows, 2 * 2**20)
    return on_device(conv_kernel, shape, cost, scratch)(
        pieces, *(jnp.asarray(table) for table in tables)
    )


def gate(q_stream, convolved, order_in, order_out):
    tok_rows, channels = q_stream.shape
    count = len(order_out)
    shape = jax.ShapeDtypeStruct((count, tok_rows // count, channels), BF16)
    cost = (q_stream.size, 6 * q_stream.size)
    kernel = functools.partial(gate_kernel, order_in, order_out)
    return on_device(kernel, shape, cost)(q_stream, convolved)


def normalize(rows, norm_gain, order):
    groups, tokens, width = rows.shape
    channels = groups * width
    shape = jax.ShapeDtypeStruct((tokens, channels), BF16)
    cost = (6 * tokens * channels, 4 * tokens * channels + 4 * channels)
    kernel = functools.partial(norm_kernel, order)
    return on_device(kernel, shape, cost)(rows, norm_gain.reshape(1, channels))


def exchange(array, axis, order):
    return lax.all_to_all(
        array, axis, split_axis=0, concat_axis=0, axis_index_groups=[order], tiled=True
    )


def far_apart(count):
    far = [0]
    while len(far) < count:
        far = [2 * n for n in far] + [2 * n + 1 for n in far]
    return far


def opposite(count):
    return [n // 2 + n % 2 * (count // 2) for n in range(count)]


def listed(places):
    return places[::-1]


def local(q_stream, k_stream, v_stream, filters, norm_gain):
    ctx, ch = lax.axis_size("ctx"), lax.axis_size("ch")
    order_in = listed(
        [
            z * 4 + (x + n) % 2 * 2 + core
            for x in range(2)
            for n, z in enumerate(far_apart(ctx // 4))
            for core in range(2)
        ]
    )
    order_back = listed(
        [
            z * 4 + (x + n) % 2 * 2 + core
            for core in range(2)
            for x in range(2)
            for n, z in enumerate(far_apart(ctx // 4))
        ]
    )
    order_ch = listed([y * 2 + x for x in range(2) for y in opposite(ch // 2)])
    pieces = exchange(mix(k_stream, v_stream, filters, order_in), "ctx", order_in)
    convolved = convolve(pieces, order_in, order_back)
    returned = exchange(convolved, "ctx", order_back)
    gated_rows = gate(q_stream, returned, order_back, order_ch)
    regrouped = exchange(gated_rows, "ch", order_ch)
    return normalize(regrouped, norm_gain, order_ch)


def solution(mesh):
    return jax.shard_map(
        local,
        mesh=mesh,
        in_specs=(P("ctx", "ch"), P("ctx", "ch"), P("ctx", "ch"), P("ctx", "ch"), P()),
        out_specs=P(("ctx", "ch"), None),
        check_vma=False,
    )
```

```python
import functools
import math

import jax
import jax.numpy as jnp
import numpy as np
from jax import lax
from jax.experimental import pallas as pl
from jax.experimental.pallas import tpu as pltpu
from jax.sharding import PartitionSpec as P

BF16 = jnp.bfloat16
F32 = jnp.float32
VMEM_BYTES = 40 * 2**20


def parts_of(table):
    high = table.astype(np.float32).astype(jnp.bfloat16)
    low = (table - high.astype(np.float64)).astype(np.float32).astype(jnp.bfloat16)
    return high, low


def stacked_table(matrix):
    table = np.block([[matrix.real, matrix.imag], [-matrix.imag, matrix.real]])
    high, low = parts_of(table)
    return np.concatenate([high, low], axis=0)


def inner_tables(tok_rows):
    half = np.arange(tok_rows // 2)
    even_turns = 2 * half[:, None] * half[None, :] % tok_rows
    odd_turns = half[:, None] * (2 * half[None, :] + 1) % tok_rows
    even, odd = (
        np.exp(-2j * np.pi * turns / tok_rows) for turns in (even_turns, odd_turns)
    )
    return stacked_table(even), stacked_table(odd), stacked_table(odd.T)


def outer_tables(blocks, tok_rows, lines, order_in, order_out):
    index = np.arange(blocks)
    freqs = np.arange(blocks + 1)
    angle = np.pi * (freqs[:, None] * index[None, :] % (2 * blocks)) / blocks
    forward = np.concatenate([np.cos(angle), -np.sin(angle)[1:blocks]], axis=0)
    weight = np.full((2 * blocks, 1), 2.0 / (2 * blocks * tok_rows))
    weight[0] *= 0.5
    weight[blocks] *= 0.5
    backward = (weight * forward).T
    apart = np.eye(lines)
    return (
        np.concatenate(parts_of(np.kron(forward[:, order_in], apart)), axis=1),
        *parts_of(np.kron(backward[order_out], apart)),
    )


def twist_tables(blocks, tok_rows):
    period = 2 * blocks * tok_rows
    index = np.arange(blocks + 1)[:, None] * np.arange(tok_rows)[None, :] % period
    angle = 2.0 * np.pi * index / period
    return np.cos(angle).astype(np.float32), np.sin(angle).astype(np.float32)


def mix_kernel(order, k_hbm, v_hbm, filters_hbm, out_ref, k_ref, v_ref, filters_ref, sems):
    groups, rows, tok_rows = out_ref.shape
    width = rows // 2
    half = tok_rows // 2
    halves = (slice(0, half), slice(half, tok_rows))
    pairs = [(k_hbm, k_ref), (v_hbm, v_ref)]
    pairs += [(filters_hbm.at[at], filters_ref.at[at]) for at in halves]
    copies = [
        pltpu.make_async_copy(source, target, sems.at[n])
        for n, (source, target) in enumerate(pairs)
    ]
    for copy in copies:
        copy.start()
    copies[0].wait()
    copies[1].wait()
    mixed = (k_ref[...].astype(F32) * v_ref[...].astype(F32)).astype(BF16)
    mixed = mixed.T.reshape(groups, width, tok_rows)
    for n, group in enumerate(order):
        out_ref[n, :width] = mixed[group]
    for at, copy in zip(halves, copies[2:]):
        copy.wait()
        taps = filters_ref[at].astype(BF16).T.reshape(groups, width, half)
        for n, group in enumerate(order):
            out_ref[n, width:, at] = taps[group]


def split_parts(values):
    high = values.astype(BF16)
    return high, (values - high.astype(F32)).astype(BF16)


def inner_dft(high, low, table_ref):
    rows = high.shape[1]
    table_high, table_low = table_ref[:rows], table_ref[rows:]
    total = jnp.dot(high, table_low, preferred_element_type=F32)
    yield total
    total = total + jnp.dot(low, table_high, preferred_element_type=F32)
    yield total
    yield total + jnp.dot(high, table_high, preferred_element_type=F32)


def side_by_side(matmuls, others):
    steps = 3 * len(matmuls)
    done, results = 0, []
    for n, matmul in enumerate(matmuls):
        for m, result in enumerate(matmul):
            upto = len(others) * (3 * n + m + 1) // steps
            for other in others[done:upto]:
                other()
            done = upto
        results.append(result)
    return results


def conv_kernel(
    in_ref, twist_ref, inner_ref, outer_ref, out_ref,
    outer, even_high, even_low, odd_high, odd_low, even, odd,
):
    blocks, rows, tok_rows = in_ref.shape
    width = rows // 2
    half = tok_rows // 2
    first, second = slice(0, half), slice(half, tok_rows)
    lines = 8
    subs = range(width // lines)
    real_rows = (blocks + 1) * lines
    cos_ref, sin_ref = twist_ref.at[0], twist_ref.at[1]
    even_ref, odd_ref, back_ref = (inner_ref.at[n] for n in range(3))
    back_rows = blocks * lines
    high_ref = outer_ref.at[2 * back_rows : 3 * back_rows]
    low_ref = outer_ref.at[3 * back_rows : 4 * back_rows]

    def of_freq(k, start=0):
        return slice(start + k * lines, start + (k + 1) * lines)

    def outer_dft(stream):
        top = stream * width
        whole = in_ref[:, top : top + width].astype(F32)
        for sub in subs:
            data = whole[:, sub * lines : (sub + 1) * lines]
            data = data.reshape(blocks * lines, tok_rows).astype(BF16)
            outer[stream, sub] = jnp.dot(
                outer_ref[: 2 * back_rows],
                jnp.concatenate([data, data], axis=0),
                preferred_element_type=F32,
            )

    def twist(stream, k):
        halves = [[], []]
        turns = [(cos_ref[k : k + 1, at], sin_ref[k : k + 1, at]) for at in (first, second)]
        for sub in subs:
            twisted = []
            for cols, (cos, sin) in zip((first, second), turns):
                re = outer[stream, sub, of_freq(k), cols]
                if k == 0:
                    twisted.append((re, jnp.zeros_like(re)))
                    continue
                if k == blocks:
                    twisted.append((re * cos, -(re * sin)))
                    continue
                im = outer[stream, sub, of_freq(k - 1, real_rows), cols]
                twisted.append((re * cos + im * sin, im * cos - re * sin))
            (re_a, im_a), (re_b, im_b) = twisted
            halves[0].append(jnp.concatenate([re_a + re_b, im_a + im_b], axis=1))
            halves[1].append(jnp.concatenate([re_a - re_b, im_a - im_b], axis=1))
        at = slice(k * width, (k + 1) * width)
        for parts, high, low in (
            (halves[0], even_high, even_low),
            (halves[1], odd_high, odd_low),
        ):
            joined = jnp.concatenate(parts, axis=0)
            high[stream, at], low[stream, at] = split_parts(joined)

    def product(sig, ker):
        sig_re, sig_im = sig[:, first], sig[:, second]
        ker_re, ker_im = ker[:, first], ker[:, second]
        prod_re = sig_re * ker_re - sig_im * ker_im
        prod_neg = -(sig_re * ker_im + sig_im * ker_re)
        return split_parts(jnp.concatenate([prod_re, prod_neg], axis=1))

    outer_dft(0)
    outer_dft(1)
    for k in range(blocks + 1):
        twist(0, k)
    sig_even, sig_odd = side_by_side(
        [
            inner_dft(even_high[0], even_low[0], even_ref),
            inner_dft(odd_high[0], odd_low[0], odd_ref),
        ],
        [functools.partial(twist, 1, k) for k in range(blocks + 1)],
    )
    made = {}

    def make(name, sig, ker):
        made[name] = product(sig, ker)

    (ker_even,) = side_by_side([inner_dft(even_high[1], even_low[1], even_ref)], [])
    (ker_odd,) = side_by_side(
        [inner_dft(odd_high[1], odd_low[1], odd_ref)],
        [functools.partial(make, "even", sig_even, ker_even)],
    )
    (even[...],) = side_by_side(
        [inner_dft(*made["even"], even_ref)],
        [functools.partial(make, "odd", sig_odd, ker_odd)],
    )
    (odd[...],) = side_by_side([inner_dft(*made["odd"], back_ref)], [])

    for k in range(blocks + 1):
        for cols, sign in ((first, 1), (second, -1)):
            cos, sin = cos_ref[k : k + 1, cols], sin_ref[k : k + 1, cols]
            for sub in subs:
                at = slice(k * width + sub * lines, k * width + (sub + 1) * lines)
                z = even[at] + odd[at] if sign > 0 else even[at] - odd[at]
                re, neg = z[:, first], z[:, second]
                outer[0, sub, of_freq(k), cols] = re * cos + neg * sin
                if 0 < k < blocks:
                    outer[0, sub, of_freq(k - 1, real_rows), cols] = re * sin - neg * cos
    parts = []
    for sub in subs:
        high, low = split_parts(outer[0, sub])
        back = jnp.dot(high_ref[...], low, preferred_element_type=F32)
        back += jnp.dot(low_ref[...], high, preferred_element_type=F32)
        back += jnp.dot(high_ref[...], high, preferred_element_type=F32)
        parts.append(back.reshape(blocks, lines, tok_rows))
    out_ref[...] = jnp.concatenate(parts, axis=1).astype(BF16)


def gate_kernel(order_in, order_out, q_ref, conv_ref, out_ref):
    groups, width, tok_rows = conv_ref.shape
    parts = [conv_ref[order_in.index(group)] for group in range(groups)]
    convolved = jnp.concatenate(parts, axis=0).T.astype(F32)
    gated_rows = (q_ref[...].astype(F32) * convolved).astype(BF16)
    tokens = out_ref.shape[1]
    for n, group in enumerate(order_out):
        out_ref[n] = gated_rows[group * tokens : (group + 1) * tokens]


def norm_kernel(order, rows_ref, gain_ref, out_ref):
    groups, _, width = rows_ref.shape
    squares = 0.0
    for n in range(groups):
        widened = rows_ref[n].astype(F32)
        squares = squares + widened * widened
    total = jnp.sum(squares, axis=1, keepdims=True)
    scaling = lax.rsqrt(total / (groups * width) + 1e-05)
    for n, group in enumerate(order):
        cols = slice(group * width, (group + 1) * width)
        row = rows_ref[n].astype(F32)
        out_ref[:, cols] = (row * scaling * gain_ref[:, cols]).astype(BF16)


def on_device(kernel, out_shape, cost, scratch=(), **specs):
    return pl.pallas_call(
        kernel,
        out_shape=out_shape,
        scratch_shapes=list(scratch),
        compiler_params=pltpu.CompilerParams(vmem_limit_bytes=VMEM_BYTES),
        cost_estimate=pl.CostEstimate(
            flops=cost[0], bytes_accessed=cost[1], transcendentals=0
        ),
        **specs,
    )


def mix(k_stream, v_stream, filters, order):
    tok_rows, channels = k_stream.shape
    groups = len(order)
    shape = jax.ShapeDtypeStruct((groups, 2 * channels // groups, tok_rows), BF16)
    cost = (k_stream.size, 12 * k_stream.size)
    scratch = [pltpu.VMEM(k_stream.shape, BF16)] * 2
    scratch += [pltpu.VMEM(k_stream.shape, F32), pltpu.SemaphoreType.DMA((4,))]
    specs = [pl.BlockSpec(memory_space=pltpu.HBM)] * 3
    held = [
        pltpu.with_memory_space_constraint(array, pltpu.HBM)
        for array in (k_stream, v_stream, filters)
    ]
    kernel = functools.partial(mix_kernel, order)
    return on_device(kernel, shape, cost, scratch, in_specs=specs)(*held)


def convolve(pieces, order_in, order_out):
    blocks, rows, tok_rows = pieces.shape
    width = rows // 2
    lines = 8
    tables = (
        np.stack(twist_tables(blocks, tok_rows)),
        np.stack(inner_tables(tok_rows)),
        np.concatenate(
            outer_tables(blocks, tok_rows, lines, order_in, order_out), axis=0
        ),
    )
    shape = jax.ShapeDtypeStruct((blocks, width, tok_rows), BF16)
    freq_rows = (blocks + 1) * width
    scratch = [pltpu.VMEM((2, width // lines, 2 * blocks * lines, tok_rows), F32)]
    scratch += [pltpu.VMEM((2, freq_rows, tok_rows), BF16)] * 4
    scratch += [pltpu.VMEM((freq_rows, tok_rows), F32)] * 2
    cost = (2 * 3 * freq_rows * 3 * 2 * tok_rows * tok_rows, 2 * 2**20)
    return on_device(conv_kernel, shape, cost, scratch)(
        pieces, *(jnp.asarray(table) for table in tables)
    )


def gate(q_stream, convolved, order_in, order_out):
    tok_rows, channels = q_stream.shape
    count = len(order_out)
    shape = jax.ShapeDtypeStruct((count, tok_rows // count, channels), BF16)
    cost = (q_stream.size, 6 * q_stream.size)
    kernel = functools.partial(gate_kernel, order_in, order_out)
    return on_device(kernel, shape, cost)(q_stream, convolved)


def normalize(rows, norm_gain, order):
    groups, tokens, width = rows.shape
    channels = groups * width
    shape = jax.ShapeDtypeStruct((tokens, channels), BF16)
    cost = (6 * tokens * channels, 4 * tokens * channels + 4 * channels)
    kernel = functools.partial(norm_kernel, order)
    return on_device(kernel, shape, cost)(rows, norm_gain.reshape(1, channels))


def exchange(array, axis, order):
    return lax.all_to_all(
        array, axis, split_axis=0, concat_axis=0, axis_index_groups=[order], tiled=True
    )


def far_apart(count):
    far = [0]
    while len(far) < count:
        far = [2 * n for n in far] + [2 * n + 1 for n in far]
    return far


def opposite(count):
    return [n // 2 + n % 2 * (count // 2) for n in range(count)]


def listed(places):
    return places[::-1]


def local(q_stream, k_stream, v_stream, filters, norm_gain):
    ctx, ch = lax.axis_size("ctx"), lax.axis_size("ch")
    order_in = listed(
        [
            z * 4 + (x + n) % 2 * 2 + core
            for x in range(2)
            for n, z in enumerate(opposite(ctx // 4))
            for core in range(2)
        ]
    )
    order_back = listed(
        [
            z * 4 + (x + n) % 2 * 2 + core
            for core in range(2)
            for x in range(2)
            for n, z in enumerate(far_apart(ctx // 4))
        ]
    )
    order_ch = listed([y * 2 + x for x in range(2) for y in opposite(ch // 2)])
    pieces = exchange(mix(k_stream, v_stream, filters, order_in), "ctx", order_in)
    convolved = convolve(pieces, order_in, order_back)
    returned = exchange(convolved, "ctx", order_back)
    gated_rows = gate(q_stream, returned, order_back, order_ch)
    regrouped = exchange(gated_rows, "ch", order_ch)
    return normalize(regrouped, norm_gain, order_ch)


def solution(mesh):
    return jax.shard_map(
        local,
        mesh=mesh,
        in_specs=(P("ctx", "ch"), P("ctx", "ch"), P("ctx", "ch"), P("ctx", "ch"), P()),
        out_specs=P(("ctx", "ch"), None),
        check_vma=False,
    )
```

```python
import functools
import math

import jax
import jax.numpy as jnp
import numpy as np
from jax import lax
from jax.experimental import pallas as pl
from jax.experimental.pallas import tpu as pltpu
from jax.sharding import PartitionSpec as P

BF16 = jnp.bfloat16
F32 = jnp.float32
VMEM_BYTES = 40 * 2**20


def parts_of(table):
    high = table.astype(np.float32).astype(jnp.bfloat16)
    low = (table - high.astype(np.float64)).astype(np.float32).astype(jnp.bfloat16)
    return high, low


def stacked_table(matrix):
    table = np.block([[matrix.real, matrix.imag], [-matrix.imag, matrix.real]])
    high, low = parts_of(table)
    return np.concatenate([high, low], axis=0)


def inner_tables(tok_rows):
    half = np.arange(tok_rows // 2)
    even_turns = 2 * half[:, None] * half[None, :] % tok_rows
    odd_turns = half[:, None] * (2 * half[None, :] + 1) % tok_rows
    even, odd = (
        np.exp(-2j * np.pi * turns / tok_rows) for turns in (even_turns, odd_turns)
    )
    return stacked_table(even), stacked_table(odd), stacked_table(odd.T)


def outer_tables(blocks, tok_rows, lines, order_in, order_out):
    index = np.arange(blocks)
    freqs = np.arange(blocks + 1)
    angle = np.pi * (freqs[:, None] * index[None, :] % (2 * blocks)) / blocks
    forward = np.concatenate([np.cos(angle), -np.sin(angle)[1:blocks]], axis=0)
    weight = np.full((2 * blocks, 1), 2.0 / (2 * blocks * tok_rows))
    weight[0] *= 0.5
    weight[blocks] *= 0.5
    backward = (weight * forward).T
    apart = np.eye(lines)
    return (
        np.concatenate(parts_of(np.kron(forward[:, order_in], apart)), axis=1),
        *parts_of(np.kron(backward[order_out], apart)),
    )


def twist_tables(blocks, tok_rows):
    period = 2 * blocks * tok_rows
    index = np.arange(blocks + 1)[:, None] * np.arange(tok_rows)[None, :] % period
    angle = 2.0 * np.pi * index / period
    return np.cos(angle).astype(np.float32), np.sin(angle).astype(np.float32)


def mix_kernel(order, k_hbm, v_hbm, filters_hbm, out_ref, k_ref, v_ref, filters_ref, sems):
    groups, rows, tok_rows = out_ref.shape
    width = rows // 2
    half = tok_rows // 2
    halves = (slice(0, half), slice(half, tok_rows))
    pairs = [(k_hbm, k_ref), (v_hbm, v_ref)]
    pairs += [(filters_hbm.at[at], filters_ref.at[at]) for at in halves]
    copies = [
        pltpu.make_async_copy(source, target, sems.at[n])
        for n, (source, target) in enumerate(pairs)
    ]
    for copy in copies:
        copy.start()
    copies[0].wait()
    copies[1].wait()
    mixed = (k_ref[...].astype(F32) * v_ref[...].astype(F32)).astype(BF16)
    mixed = mixed.T.reshape(groups, width, tok_rows)
    for n, group in enumerate(order):
        out_ref[n, :width] = mixed[group]
    for at, copy in zip(halves, copies[2:]):
        copy.wait()
        taps = filters_ref[at].astype(BF16).T.reshape(groups, width, half)
        for n, group in enumerate(order):
            out_ref[n, width:, at] = taps[group]


def split_parts(values):
    high = values.astype(BF16)
    return high, (values - high.astype(F32)).astype(BF16)


def inner_dft(high, low, table_ref):
    rows = high.shape[1]
    table_high, table_low = table_ref[:rows], table_ref[rows:]
    total = jnp.dot(high, table_low, preferred_element_type=F32)
    yield total
    total = total + jnp.dot(low, table_high, preferred_element_type=F32)
    yield total
    yield total + jnp.dot(high, table_high, preferred_element_type=F32)


def side_by_side(matmuls, others):
    steps = 3 * len(matmuls)
    done, results = 0, []
    for n, matmul in enumerate(matmuls):
        for m, result in enumerate(matmul):
            upto = len(others) * (3 * n + m + 1) // steps
            for other in others[done:upto]:
                other()
            done = upto
        results.append(result)
    return results


def conv_kernel(
    in_ref, twist_ref, inner_ref, outer_ref, out_ref,
    outer, even_high, even_low, odd_high, odd_low, even, odd,
):
    blocks, rows, tok_rows = in_ref.shape
    width = rows // 2
    half = tok_rows // 2
    first, second = slice(0, half), slice(half, tok_rows)
    lines = 8
    subs = range(width // lines)
    real_rows = (blocks + 1) * lines
    cos_ref, sin_ref = twist_ref.at[0], twist_ref.at[1]
    even_ref, odd_ref, back_ref = (inner_ref.at[n] for n in range(3))
    back_rows = blocks * lines
    high_ref = outer_ref.at[2 * back_rows : 3 * back_rows]
    low_ref = outer_ref.at[3 * back_rows : 4 * back_rows]

    def of_freq(k, start=0):
        return slice(start + k * lines, start + (k + 1) * lines)

    def outer_dft(stream):
        top = stream * width
        whole = in_ref[:, top : top + width].astype(F32)
        for sub in subs:
            data = whole[:, sub * lines : (sub + 1) * lines]
            data = data.reshape(blocks * lines, tok_rows).astype(BF16)
            outer[stream, sub] = jnp.dot(
                outer_ref[: 2 * back_rows],
                jnp.concatenate([data, data], axis=0),
                preferred_element_type=F32,
            )

    def twist(stream, k):
        halves = [[], []]
        turns = [(cos_ref[k : k + 1, at], sin_ref[k : k + 1, at]) for at in (first, second)]
        for sub in subs:
            twisted = []
            for cols, (cos, sin) in zip((first, second), turns):
                re = outer[stream, sub, of_freq(k), cols]
                if k == 0:
                    twisted.append((re, jnp.zeros_like(re)))
                    continue
                if k == blocks:
                    twisted.append((re * cos, -(re * sin)))
                    continue
                im = outer[stream, sub, of_freq(k - 1, real_rows), cols]
                twisted.append((re * cos + im * sin, im * cos - re * sin))
            (re_a, im_a), (re_b, im_b) = twisted
            halves[0].append(jnp.concatenate([re_a + re_b, im_a + im_b], axis=1))
            halves[1].append(jnp.concatenate([re_a - re_b, im_a - im_b], axis=1))
        at = slice(k * width, (k + 1) * width)
        for parts, high, low in (
            (halves[0], even_high, even_low),
            (halves[1], odd_high, odd_low),
        ):
            joined = jnp.concatenate(parts, axis=0)
            high[stream, at], low[stream, at] = split_parts(joined)

    def product(sig, ker):
        sig_re, sig_im = sig[:, first], sig[:, second]
        ker_re, ker_im = ker[:, first], ker[:, second]
        prod_re = sig_re * ker_re - sig_im * ker_im
        prod_neg = -(sig_re * ker_im + sig_im * ker_re)
        return split_parts(jnp.concatenate([prod_re, prod_neg], axis=1))

    outer_dft(0)
    outer_dft(1)
    for k in range(blocks + 1):
        twist(0, k)
    sig_even, sig_odd = side_by_side(
        [
            inner_dft(even_high[0], even_low[0], even_ref),
            inner_dft(odd_high[0], odd_low[0], odd_ref),
        ],
        [functools.partial(twist, 1, k) for k in range(blocks + 1)],
    )
    made = {}

    def make(name, sig, ker):
        made[name] = product(sig, ker)

    (ker_even,) = side_by_side([inner_dft(even_high[1], even_low[1], even_ref)], [])
    (ker_odd,) = side_by_side(
        [inner_dft(odd_high[1], odd_low[1], odd_ref)],
        [functools.partial(make, "even", sig_even, ker_even)],
    )
    (even[...],) = side_by_side(
        [inner_dft(*made["even"], even_ref)],
        [functools.partial(make, "odd", sig_odd, ker_odd)],
    )
    (odd[...],) = side_by_side([inner_dft(*made["odd"], back_ref)], [])

    for k in range(blocks + 1):
        for cols, sign in ((first, 1), (second, -1)):
            cos, sin = cos_ref[k : k + 1, cols], sin_ref[k : k + 1, cols]
            for sub in subs:
                at = slice(k * width + sub * lines, k * width + (sub + 1) * lines)
                z = even[at] + odd[at] if sign > 0 else even[at] - odd[at]
                re, neg = z[:, first], z[:, second]
                outer[0, sub, of_freq(k), cols] = re * cos + neg * sin
                if 0 < k < blocks:
                    outer[0, sub, of_freq(k - 1, real_rows), cols] = re * sin - neg * cos
    parts = []
    for sub in subs:
        high, low = split_parts(outer[0, sub])
        back = jnp.dot(high_ref[...], low, preferred_element_type=F32)
        back += jnp.dot(low_ref[...], high, preferred_element_type=F32)
        back += jnp.dot(high_ref[...], high, preferred_element_type=F32)
        parts.append(back.reshape(blocks, lines, tok_rows))
    out_ref[...] = jnp.concatenate(parts, axis=1).astype(BF16)


def gate_kernel(order_in, order_out, q_ref, conv_ref, out_ref):
    groups, width, tok_rows = conv_ref.shape
    parts = [conv_ref[order_in.index(group)] for group in range(groups)]
    convolved = jnp.concatenate(parts, axis=0).T.astype(F32)
    gated_rows = (q_ref[...].astype(F32) * convolved).astype(BF16)
    tokens = out_ref.shape[1]
    for n, group in enumerate(order_out):
        out_ref[n] = gated_rows[group * tokens : (group + 1) * tokens]


def norm_kernel(order, rows_ref, gain_ref, out_ref):
    groups, _, width = rows_ref.shape
    squares = 0.0
    for n in range(groups):
        widened = rows_ref[n].astype(F32)
        squares = squares + widened * widened
    total = jnp.sum(squares, axis=1, keepdims=True)
    scaling = lax.rsqrt(total / (groups * width) + 1e-05)
    for n, group in enumerate(order):
        cols = slice(group * width, (group + 1) * width)
        row = rows_ref[n].astype(F32)
        out_ref[:, cols] = (row * scaling * gain_ref[:, cols]).astype(BF16)


def on_device(kernel, out_shape, cost, scratch=(), **specs):
    return pl.pallas_call(
        kernel,
        out_shape=out_shape,
        scratch_shapes=list(scratch),
        compiler_params=pltpu.CompilerParams(vmem_limit_bytes=VMEM_BYTES),
        cost_estimate=pl.CostEstimate(
            flops=cost[0], bytes_accessed=cost[1], transcendentals=0
        ),
        **specs,
    )


def mix(k_stream, v_stream, filters, order):
    tok_rows, channels = k_stream.shape
    groups = len(order)
    shape = jax.ShapeDtypeStruct((groups, 2 * channels // groups, tok_rows), BF16)
    cost = (k_stream.size, 12 * k_stream.size)
    scratch = [pltpu.VMEM(k_stream.shape, BF16)] * 2
    scratch += [pltpu.VMEM(k_stream.shape, F32), pltpu.SemaphoreType.DMA((4,))]
    specs = [pl.BlockSpec(memory_space=pltpu.HBM)] * 3
    held = [
        pltpu.with_memory_space_constraint(array, pltpu.HBM)
        for array in (k_stream, v_stream, filters)
    ]
    kernel = functools.partial(mix_kernel, order)
    return on_device(kernel, shape, cost, scratch, in_specs=specs)(*held)


def convolve(pieces, order_in, order_out):
    blocks, rows, tok_rows = pieces.shape
    width = rows // 2
    lines = 8
    tables = (
        np.stack(twist_tables(blocks, tok_rows)),
        np.stack(inner_tables(tok_rows)),
        np.concatenate(
            outer_tables(blocks, tok_rows, lines, order_in, order_out), axis=0
        ),
    )
    shape = jax.ShapeDtypeStruct((blocks, width, tok_rows), BF16)
    freq_rows = (blocks + 1) * width
    scratch = [pltpu.VMEM((2, width // lines, 2 * blocks * lines, tok_rows), F32)]
    scratch += [pltpu.VMEM((2, freq_rows, tok_rows), BF16)] * 4
    scratch += [pltpu.VMEM((freq_rows, tok_rows), F32)] * 2
    cost = (2 * 3 * freq_rows * 3 * 2 * tok_rows * tok_rows, 2 * 2**20)
    return on_device(conv_kernel, shape, cost, scratch)(
        pieces, *(jnp.asarray(table) for table in tables)
    )


def gate(q_stream, convolved, order_in, order_out):
    tok_rows, channels = q_stream.shape
    count = len(order_out)
    shape = jax.ShapeDtypeStruct((count, tok_rows // count, channels), BF16)
    cost = (q_stream.size, 6 * q_stream.size)
    kernel = functools.partial(gate_kernel, order_in, order_out)
    return on_device(kernel, shape, cost)(q_stream, convolved)


def normalize(rows, norm_gain, order):
    groups, tokens, width = rows.shape
    channels = groups * width
    shape = jax.ShapeDtypeStruct((tokens, channels), BF16)
    cost = (6 * tokens * channels, 4 * tokens * channels + 4 * channels)
    kernel = functools.partial(norm_kernel, order)
    return on_device(kernel, shape, cost)(rows, norm_gain.reshape(1, channels))


def exchange(array, axis, order):
    return lax.all_to_all(
        array, axis, split_axis=0, concat_axis=0, axis_index_groups=[order], tiled=True
    )


def far_apart(count):
    far = [0]
    while len(far) < count:
        far = [2 * n for n in far] + [2 * n + 1 for n in far]
    return far


def opposite(count):
    return [n // 2 + n % 2 * (count // 2) for n in range(count)]


def listed(places):
    return places[::-1]


def local(q_stream, k_stream, v_stream, filters, norm_gain):
    ctx, ch = lax.axis_size("ctx"), lax.axis_size("ch")
    order_in = listed(
        [
            z * 4 + (x + n) % 2 * 2 + core
            for x in range(2)
            for n, z in enumerate(far_apart(ctx // 4))
            for core in range(2)
        ]
    )
    order_back = listed(
        [
            z * 4 + (x + n) % 2 * 2 + core
            for core in range(2)
            for x in range(2)
            for n, z in enumerate(far_apart(ctx // 4))
        ]
    )
    planes = opposite(ch // 2)
    rounds = (planes[: ch // 4], planes[ch // 4 :])
    order_ch = listed([y * 2 + x for part in rounds for x in range(2) for y in part])
    pieces = exchange(mix(k_stream, v_stream, filters, order_in), "ctx", order_in)
    convolved = convolve(pieces, order_in, order_back)
    returned = exchange(convolved, "ctx", order_back)
    gated_rows = gate(q_stream, returned, order_back, order_ch)
    regrouped = exchange(gated_rows, "ch", order_ch)
    return normalize(regrouped, norm_gain, order_ch)


def solution(mesh):
    return jax.shard_map(
        local,
        mesh=mesh,
        in_specs=(P("ctx", "ch"), P("ctx", "ch"), P("ctx", "ch"), P("ctx", "ch"), P()),
        out_specs=P(("ctx", "ch"), None),
        check_vma=False,
    )
```
